32 devices in a mesh: groups: 2 (over y), seq: 4 (over z), chan: 2 (over x), dp: 2 (over core).
Axes of the slice: x: 2, y: 2, z: 4, core: 2. Of those that a mesh axis runs over, the one named last changes fastest.
Arguments:
- conv_input: bfloat16 [4, 2048, 2048], P(('groups', 'dp'), 'seq', 'chan'), parts along dimension 0, may hold values from -6 to 6
- conv_weight: float32 [4, 2048], P(None, 'chan'), may hold values from -3 to 3
- log_decay: float32 [4, 2048, 32], P(('groups', 'dp'), 'seq', 'chan'), parts along dimension 0, as said below
- state_in: bfloat16 [4, 2048, 128], P(('groups', 'dp'), 'seq'), parts along dimension 0, may hold values from -1.5 to 1.5
- state_out: bfloat16 [4, 2048, 128], P(('groups', 'dp'), 'seq'), parts along dimension 0, may hold values from -1.5 to 1.5
- out_grad: bfloat16 [4, 2048, 2048], P(('groups', 'dp'), 'seq', 'chan'), parts along dimension 0, may hold values from -3 to 3
- lengths: int32 [4], P(('groups', 'dp')), parts along dimension 0, may hold values from 1 to 2048, as said below
- segment_starts: int32 [4, 2], P(('groups', 'dp')), parts along dimension 0, may hold values from 1 to 2047
Outputs:
- input_grad: bfloat16 [4, 2048, 2048], P(('groups', 'dp'), 'seq', 'chan'), parts along dimension 0
- state_in_grad: float32 [4, 2048, 128], P(('groups', 'dp'), 'seq'), parts along dimension 0
- state_out_grad: float32 [4, 2048, 128], P(('groups', 'dp'), 'seq'), parts along dimension 0
- weight_grad: float32 [8, 2048], P('groups', 'chan'), parts along dimension 0
The draws below stay inside these ranges and needn't reach their ends.
There are 2 independent parts, one for each index of `groups`. The reference program is written for one: setup_inputs(seed, part) draws one part's arguments, and reference() takes and returns one part's arrays. A program takes and returns all parts, laid end to end along the dimension named above; an argument that names none is the same for every part. Nothing has to cross between parts.
Inputs may be any that keep to these rules, and one draw needn't show every extreme that they name: `lengths`: at least one series of a group runs the full 2048 steps. `log_decay`: strictly negative.
All inputs are finite; a program needn't handle non-finite values.
Results may differ from the reference program's by a relative error of at most 0.019.
Values may be sent and summed in bfloat16 or wider, within the bound.
A program may use at most 128 MiB of HBM per device.

```python
import math
import jax
import jax.numpy as jnp
from jax import lax

N = 128
BLOCK = 256
KERNEL = 4
STARTS = 2
LEN_DEV = 512
SERIES_LENGTH = 2048
SERIES_COUNT = 2
HEAD_COUNT = 32
CH = 2048


def draw_log_decay(key, part):
    random_keys = jax.random.split(key, 7)
    share = 0.5
    fast = jax.random.uniform(random_keys[0], (HEAD_COUNT,)) < share
    fast_rate = jnp.exp(jax.random.uniform(random_keys[1], (HEAD_COUNT,), minval=math.log(1.0 / 50.0), maxval=math.log(1.0 / 30.0)))
    slow_rate = jnp.exp(jax.random.uniform(random_keys[2], (HEAD_COUNT,), minval=math.log(0.05), maxval=math.log(0.4))) / SERIES_LENGTH
    rate = jnp.where(fast, fast_rate, slow_rate)
    pieces = SERIES_LENGTH // LEN_DEV
    factor = jnp.exp(jax.random.uniform(random_keys[3], (SERIES_COUNT, pieces, 1, HEAD_COUNT), minval=math.log(0.7), maxval=math.log(1.4)))
    factor = jnp.broadcast_to(factor, (SERIES_COUNT, pieces, LEN_DEV, HEAD_COUNT)).reshape(SERIES_COUNT, SERIES_LENGTH, HEAD_COUNT)
    rough = jnp.clip(1.0 + 0.25 * jax.random.normal(random_keys[4], (SERIES_COUNT, SERIES_LENGTH, HEAD_COUNT)), 0.6, 1.4)
    spike_index = jax.random.randint(random_keys[5], (SERIES_COUNT, 2), 0, SERIES_LENGTH)
    spike_mask = jnp.log(jax.random.uniform(random_keys[6], (SERIES_COUNT, 2, HEAD_COUNT), minval=0.5, maxval=0.8))
    match_mask = jnp.arange(SERIES_LENGTH)[None, :, None] == spike_index[:, None, :]
    additional_term = jnp.sum(jnp.where(match_mask[..., None], spike_mask[:, None, :, :], 0.0), axis=2)
    return (-rate * factor * rough + additional_term).astype(jnp.float32)


def draw_lengths(key, part):
    drawn = jax.random.randint(key, (SERIES_COUNT,), 1, SERIES_LENGTH + 1)
    chosen = jax.random.randint(jax.random.fold_in(key, 7), (), 0, SERIES_COUNT)
    return jnp.where(jnp.arange(SERIES_COUNT) == chosen, SERIES_LENGTH, drawn).astype(jnp.int32)


def with_ends(entries, key, smallest, largest):
    spot = [jax.random.randint(jax.random.fold_in(key, axis), (), 0, length) for axis, length in enumerate(entries.shape)]
    main_axis = entries.shape.index(max(entries.shape))
    next_to = spot[:main_axis] + [(spot[main_axis] + 1) % entries.shape[main_axis]] + spot[main_axis + 1:]
    return entries.at[tuple(spot)].set(smallest).at[tuple(next_to)].set(largest)


def shard_levels(rng, shape, shards, least, top_value):
    factor_of = 1.0
    for dim, blocks in shards:
        draws = jax.random.uniform(jax.random.fold_in(jax.random.fold_in(rng, 6), dim), (blocks,), jnp.float32, least / len(shards), top_value / len(shards))
        factor_of = factor_of * jnp.repeat(jnp.exp(draws), shape[dim] // blocks).reshape((-1,) + (1,) * (len(shape) - 1 - dim))
    return factor_of


def scatter_about(own_key, dims, scale, most, cuts=(), kind=jnp.bfloat16):
    level = shard_levels(own_key, dims, cuts, -0.22, 0.18) if cuts else 1.0
    values = jax.random.normal(own_key, dims, jnp.float32) * scale * level
    return jnp.minimum(jnp.maximum(values, -most), most).astype(kind)


def setup_inputs(seed: int = 0, part: int = 0) -> dict:
    key_list = jax.random.split(jax.random.key(seed), 9)
    part_splits = jax.random.split(jax.random.fold_in(key_list[8], part), 9)
    return {
        "conv_input": scatter_about(part_splits[0], (SERIES_COUNT, SERIES_LENGTH, CH), 1.0, 6.0, ((0, 2), (1, 4), (2, 2))),
        "conv_weight": scatter_about(key_list[1], (KERNEL, CH), KERNEL ** -0.5, 3.0, ((1, 2),), jnp.float32),
        "log_decay": draw_log_decay(jax.random.fold_in(jax.random.fold_in(key_list[8], part), 71), part),
        "state_in": scatter_about(part_splits[3], (SERIES_COUNT, SERIES_LENGTH, N), 0.25, 1.5, ((0, 2), (1, 4))),
        "state_out": scatter_about(part_splits[4], (SERIES_COUNT, SERIES_LENGTH, N), 0.25, 1.5, ((0, 2), (1, 4))),
        "out_grad": scatter_about(part_splits[5], (SERIES_COUNT, SERIES_LENGTH, CH), 0.5, 3.0, ((0, 2), (1, 4), (2, 2))),
        "lengths": draw_lengths(jax.random.fold_in(jax.random.fold_in(key_list[8], part), 71), part),
        "segment_starts": with_ends(jax.random.randint(part_splits[7], (SERIES_COUNT, STARTS), 1, SERIES_LENGTH), jax.random.fold_in(part_splits[7], 1), 1, SERIES_LENGTH - 1).astype(jnp.int32),
    }


HIGH = lax.Precision.HIGHEST

def block_decay(logs, resets, full):
    kept = jnp.where(resets[:, :, None], jnp.float32(0.0), logs)
    running = jnp.cumsum(kept, axis=1)
    segment = jnp.cumsum(resets.astype(jnp.int32), axis=1)
    steps = logs.shape[1]
    order = jnp.arange(steps, dtype=jnp.int32)
    final = running[:, -1:, :]
    final_seg = segment[:, -1:]
    start_decay = jnp.where((segment == 0)[:, :, None], jnp.exp(running), jnp.float32(0.0))
    end_decay = jnp.where((segment == final_seg)[:, :, None], jnp.exp(final - running), jnp.float32(0.0))
    whole = jnp.where(final_seg == 0, jnp.exp(final[:, 0, :]), jnp.float32(0.0))
    if not full:
        return (start_decay, end_decay, whole)
    per_head = jnp.transpose(running, (0, 2, 1))
    spread = per_head[:, :, :, None] - per_head[:, :, None, :]
    linked = (segment[:, :, None] == segment[:, None, :]) & (order[:, None] >= order[None, :])[None]
    linked = linked[:, None]
    decay_map = jnp.where(linked, jnp.exp(jnp.where(linked, spread, jnp.float32(0.0))), jnp.float32(0.0))
    return (decay_map, start_decay, end_decay, whole)

def block_state(values, matrix, decay):
    return jnp.einsum('bsh,bshp,bsn->bhpn', decay, values.astype(jnp.float32), matrix.astype(jnp.float32), precision=HIGH)

def block_outputs(scan_in, masked, in_mat, out_mat, decay_map, start_decay, end_decay, state, grad_state):
    scan_f = scan_in.astype(jnp.float32)
    grads_f = masked.astype(jnp.float32)
    in_f = in_mat.astype(jnp.float32)
    out_f = out_mat.astype(jnp.float32)
    scores = jnp.einsum('bthp,bshp->bhts', grads_f, scan_f, precision=HIGH)
    weighted = lax.optimization_barrier((scores * decay_map).astype(jnp.bfloat16)).astype(jnp.float32)
    inner = jnp.einsum('btn,bsn->bts', out_f, in_f, precision=HIGH)
    carried = lax.optimization_barrier((inner[:, None] * decay_map).astype(jnp.bfloat16)).astype(jnp.float32)
    out_part = jnp.einsum('bhts,bsn->btn', weighted, in_f, precision=HIGH)
    out_part = out_part + jnp.einsum('bth,bthn->btn', start_decay, jnp.einsum('bthp,bhpn->bthn', grads_f, state, precision=HIGH), precision=HIGH)
    in_part = jnp.einsum('bhrt,brn->btn', weighted, out_f, precision=HIGH)
    in_part = in_part + jnp.einsum('bth,bthn->btn', end_decay, jnp.einsum('bthp,bhpn->bthn', scan_f, grad_state, precision=HIGH), precision=HIGH)
    scan_grad = jnp.einsum('bhrt,brhp->bthp', carried, grads_f, precision=HIGH)
    scan_grad = scan_grad + end_decay[..., None] * jnp.einsum('bhpn,btn->bthp', grad_state, in_f, precision=HIGH)
    return (out_part, in_part, scan_grad)

def blocked(array, count):
    shape = array.shape
    grouped = array.reshape((shape[0], count, shape[1] // count) + shape[2:])
    return jnp.swapaxes(grouped, 0, 1)

def unblocked(array):
    shape = array.shape
    joined = jnp.swapaxes(array, 0, 1)
    return joined.reshape((shape[1], shape[0] * shape[2]) + shape[3:])

def reference(conv_input, conv_weight, log_decay, state_in, state_out, out_grad, lengths, segment_starts):
    batch, total, channels = conv_input.shape
    heads = log_decay.shape[2]
    width = channels // heads
    states = state_in.shape[2]
    kernel = conv_weight.shape[0]
    position = jnp.arange(total, dtype=jnp.int32)
    valid = (position[None, :] < lengths[:, None])[:, :, None]
    resets = jnp.any(segment_starts[:, None, :] == position[None, :, None], axis=2)
    padded = jnp.concatenate([jnp.zeros((batch, kernel - 1, channels), conv_input.dtype), conv_input], axis=1)
    mixed = jnp.zeros((batch, total, channels), jnp.float32)
    for offset in range(kernel):
        mixed = mixed + conv_weight[offset] * padded[:, offset:offset + total].astype(jnp.float32)
    gain = jnp.where(resets[:, :, None], jnp.float32(1.0), jnp.sqrt(-jnp.expm1(2.0 * log_decay)))
    sigmoid_u = jax.nn.sigmoid(mixed)
    activated = ((mixed * sigmoid_u).reshape(batch, total, heads, width) * gain[..., None]).reshape(batch, total, channels)
    scan_in = jnp.where(valid, activated, jnp.float32(0.0)).astype(jnp.bfloat16).reshape(batch, total, heads, width)
    masked = jnp.where(valid, out_grad, jnp.zeros_like(out_grad)).reshape(batch, total, heads, width)
    count = total // BLOCK
    scan_blocks = blocked(scan_in, count)
    grad_blocks = blocked(masked, count)
    in_blocks = blocked(state_in, count)
    out_blocks = blocked(state_out, count)
    log_blocks = blocked(log_decay, count)
    reset_blocks = blocked(resets, count)
    zero_state = jnp.zeros((batch, heads, width, states), jnp.float32)

    def forward(carry, item):
        values, matrix, logs, marks = item
        start_decay, end_decay, whole = block_decay(logs, marks, False)
        return (whole[:, :, None, None] * carry + block_state(values, matrix, end_decay), carry)
    _, entering = lax.scan(forward, zero_state, (scan_blocks, in_blocks, log_blocks, reset_blocks))

    def backward(carry, item):
        values, matrix, logs, marks = item
        start_decay, end_decay, whole = block_decay(logs, marks, False)
        return (whole[:, :, None, None] * carry + block_state(values, matrix, start_decay), carry)
    _, leaving = lax.scan(backward, zero_state, (grad_blocks, out_blocks, log_blocks, reset_blocks), reverse=True)

    def per_block(item):
        values, grads, in_b, out_b, logs, marks, state, grad_state = item
        decay_map, start_decay, end_decay, whole = block_decay(logs, marks, True)
        return block_outputs(values, grads, in_b, out_b, decay_map, start_decay, end_decay, state, grad_state)
    out_parts, in_parts, scan_grads = lax.map(per_block, (scan_blocks, grad_blocks, in_blocks, out_blocks, log_blocks, reset_blocks, entering, leaving))
    state_out_grad = unblocked(out_parts)
    state_in_grad = unblocked(in_parts)
    scan_grad = unblocked(scan_grads)
    slope = sigmoid_u * (1.0 + mixed * (1.0 - sigmoid_u))
    mixed_grad = (scan_grad * gain[..., None]).reshape(batch, total, channels) * slope
    mixed_grad = jnp.where(valid, mixed_grad, jnp.float32(0.0)).astype(jnp.bfloat16)
    grad_pad = jnp.concatenate([mixed_grad, jnp.zeros((batch, kernel - 1, channels), jnp.bfloat16)], axis=1)
    input_grad = jnp.zeros((batch, total, channels), jnp.float32)
    for offset in range(kernel):
        start = kernel - 1 - offset
        input_grad = input_grad + conv_weight[offset] * grad_pad[:, start:start + total].astype(jnp.float32)
    input_grad = input_grad.astype(jnp.bfloat16)
    wide_grad = mixed_grad.astype(jnp.float32)
    rows = []
    for offset in range(kernel):
        rows.append(lax.optimization_barrier(jnp.sum(wide_grad * padded[:, offset:offset + total].astype(jnp.float32), axis=(0, 1))))
    weight_grad = jnp.stack(rows) / jnp.sqrt(jnp.float32(batch * total))
    return (input_grad, state_in_grad, state_out_grad, weight_grad)
```

```python
import functools
import math

import jax
import jax.numpy as jnp
from jax import lax
from jax.experimental import pallas as pl
from jax.experimental.pallas import tpu as pltpu
from jax.sharding import PartitionSpec as P

BLOCK = 256
GROUP = 256
F32 = jnp.float32
BF16 = jnp.bfloat16
MESH = pl.DeviceIdType.MESH
LANES = (((1,), (1,)), ((), ()))


def dot(a, b):
    return jnp.dot(a, b, preferred_element_type=F32)


def dot_lanes(a, b):
    return lax.dot_general(a, b, LANES, preferred_element_type=F32)


def iota(shape, dim):
    return lax.broadcasted_iota(jnp.int32, shape, dim)


def pack(values):
    upper = values.astype(BF16)
    lower = (values - upper.astype(F32)).astype(BF16)
    return jnp.concatenate([upper, lower], axis=1)


def one_minus_exp(y):
    series = 1.0 / 5040.0
    for term in (720.0, 120.0, 24.0, 6.0, 2.0, 1.0):
        series = series * y + 1.0 / term
    return jnp.where(y > -0.35, -y * series, 1.0 - jnp.exp(y))


def kernel(
    seq_n, chan_n, dp_n,
    x_ref, w_ref, ld_ref, bi_ref, co_ref, og_ref, len_ref, st_ref,
    ig_ref, sig_ref, sog_ref, wg_ref,
    rim_in, xpad, mgpad, gs, ee, sgrad, colb, rowb, mask, inner, wsum,
    packs, whole, scan, sg, ss, push, pull, lead,
    f_out, f_in, b_out, b_in, cbuf, mg_out, mg_in, wbuf,
    x_sem, f_sem, b_sem, m_sem, c_send, c_recv, w_send, w_recv,
):
    local, channels = x_ref.shape
    heads = ld_ref.shape[1]
    width = channels // heads
    taps = w_ref.shape[0]
    blocks = local // BLOCK
    groups = channels // GROUP
    pairs = channels // 128
    per = 128 // width
    starts = st_ref.shape[1]
    team = seq_n * dp_n
    seq = lax.axis_index("seq")
    chan = lax.axis_index("chan")
    core = lax.axis_index("dp")
    mine = seq * dp_n + core

    def member(step):
        other = lax.rem(mine + step, team)
        return {"seq": lax.div(other, dp_n), "dp": lax.rem(other, dp_n)}

    def peer(step):
        return {"chan": lax.rem(chan + step, chan_n)}

    barrier = pltpu.get_barrier_semaphore()

    def greet(step, carry):
        pl.semaphore_signal(barrier, inc=1, device_id=member(step), device_id_type=MESH)
        return carry

    lax.fori_loop(1, team, greet, 0)
    for step in range(1, chan_n):
        pl.semaphore_signal(barrier, inc=1, device_id=peer(step), device_id_type=MESH)

    def remote(src, dst, send, recv, target):
        return pltpu.make_async_remote_copy(
            src_ref=src, dst_ref=dst, send_sem=send, recv_sem=recv,
            device_id=target, device_id_type=MESH,
        )

    def spans(b):
        return pl.ds(b * BLOCK, BLOCK)

    length = len_ref[0]
    for b in range(blocks):
        base = seq * local + b * BLOCK
        shape = (BLOCK, heads)
        place = base + iota(shape, 0)
        reset = place == st_ref[0, 0]
        for j in range(1, starts):
            reset = reset | (place == st_ref[0, j])

        def segments(pos):
            total = jnp.zeros(pos.shape, jnp.int32)
            for j in range(starts):
                begin = st_ref[0, j]
                total = total + ((pos >= begin) & (base <= begin)).astype(jnp.int32)
            return total

        segment = segments(place)
        logs = ld_ref[spans(b), :]
        kept = jnp.where(reset, 0.0, logs)
        order_r = iota((BLOCK, BLOCK), 0)
        order_c = iota((BLOCK, BLOCK), 1)
        tri = (order_r >= order_c).astype(F32)
        running = lax.dot_general(
            tri, kept, (((1,), (0,)), ((), ())),
            precision=lax.Precision.HIGHEST, preferred_element_type=F32,
        )
        final = running[BLOCK - 1 :, :]
        start = jnp.where(segment == 0, jnp.exp(running), 0.0)
        end = jnp.where(segment == segment[BLOCK - 1 :, :], jnp.exp(final - running), 0.0)
        valid = place < length
        gain = jnp.where(reset, 1.0, jnp.sqrt(one_minus_exp(2.0 * logs)))
        packs[0, spans(b), :] = pack(jnp.where(valid, start, 0.0))
        packs[1, spans(b), :] = pack(end)
        packs[2, spans(b), :] = pack(jnp.where(valid, gain, 0.0))
        last = jnp.broadcast_to(start[BLOCK - 1 :, :], (16, heads))
        spread_e = (lax.rem(iota((2 * heads, channels), 0), heads)
                    == lax.div(iota((2 * heads, channels), 1), width)).astype(BF16)
        whole[b] = dot(pack(last), spread_e)[:8]
        turned = jnp.transpose(running)
        for h in range(heads):
            colb[h, spans(b), :] = jnp.broadcast_to(running[:, h : h + 1], (BLOCK, 128))
            rowb[b, h] = turned[h : h + 1, :]
        pos_s = base + order_r
        pos_t = base + order_c
        linked = (order_c >= order_r) & (segments(pos_s) == segments(pos_t)) & (pos_t < length)
        mask[b] = jnp.where(linked, 0.0, -jnp.inf)
        inner[b] = dot_lanes(bi_ref[spans(b), :], co_ref[spans(b), :])
        wsum[b] = jnp.zeros((BLOCK, BLOCK), F32)

    def lanes(g):
        return pl.ds(pl.multiple_of(g * GROUP, GROUP), GROUP)

    def spread(g):
        shape = (2 * heads, GROUP)
        head = lax.rem(iota(shape, 0), heads)
        return (head == lax.div(iota(shape, 1) + g * GROUP, width)).astype(BF16)

    pl.semaphore_wait(barrier, team - 1 + chan_n - 1)

    tail = pl.ds(local - 16, 16)

    def rim_copy():
        return remote(x_ref.at[tail], rim_in, x_sem.at[0], x_sem.at[1], {"seq": seq + 1})

    @pl.when(seq < seq_n - 1)
    def _():
        rim_copy().start()

    def f_copy(c):
        return remote(f_out.at[c], f_in.at[c], f_sem.at[0, c], f_sem.at[1, c], {"seq": seq + 1})

    def b_copy(c):
        return remote(b_out.at[c], b_in.at[c], b_sem.at[0, c], b_sem.at[1, c], {"seq": seq - 1})

    def advance(c):
        state = f_in[c].astype(F32)
        for b in range(blocks):
            state = whole[b, 0:1, lanes(c)] * state + push[b, c]
        f_out[c] = state.astype(BF16)

    def retreat(c):
        state = b_in[c].astype(F32)
        for b in reversed(range(blocks)):
            state = whole[b, 0:1, lanes(c)] * state + pull[b, c]
        b_out[c] = state.astype(BF16)

    outs_t = [jnp.transpose(co_ref[spans(b), :].astype(F32)).astype(BF16) for b in range(blocks)]

    @pl.when(seq == seq_n - 1)
    def _():
        b_in[...] = jnp.zeros(b_in.shape, BF16)

    def pulled(g, carry):
        e = spread(g)
        for b in range(blocks):
            scaled = (dot(packs[0, spans(b), :], e) * og_ref[spans(b), lanes(g)].astype(F32)).astype(BF16)
            sg[spans(b), lanes(g)] = scaled
            pull[b, g] = dot(outs_t[b], scaled)

        @pl.when((seq == seq_n - 1) & (seq > 0))
        def _():
            retreat(g)
            b_copy(g).start()

        return carry

    lax.fori_loop(0, groups, pulled, 0)

    xpad[pl.ds(8, local), :] = x_ref[...].astype(F32)

    @pl.when(seq == 0)
    def _():
        xpad[pl.ds(0, 8), :] = jnp.zeros((8, channels), F32)
        f_in[...] = jnp.zeros(f_in.shape, BF16)

    @pl.when(seq > 0)
    def _():
        rim_copy().wait_recv()
        xpad[pl.ds(0, 8), :] = rim_in[...].astype(F32)[8:]

    ins_t = [jnp.transpose(bi_ref[spans(b), :].astype(F32)).astype(BF16) for b in range(blocks)]

    def shifted(b, k, g):
        return xpad[pl.ds(8 + b * BLOCK - (taps - 1) + k, BLOCK), lanes(g)]

    def pushed(g, carry):
        e = spread(g)
        for b in range(blocks):
            mixed = w_ref[0:1, lanes(g)] * shifted(b, 0, g)
            for k in range(1, taps):
                mixed = mixed + w_ref[k : k + 1, lanes(g)] * shifted(b, k, g)
            gate = 0.5 + 0.5 * jnp.tanh(0.5 * mixed)
            gain = dot(packs[2, spans(b), :], e)
            end = dot(packs[1, spans(b), :], e)
            act = (mixed * gate * gain).astype(BF16)
            scan[spans(b), lanes(g)] = act
            gs[spans(b), lanes(g)] = gain * gate * (1.0 + mixed * (1.0 - gate))
            ee[spans(b), lanes(g)] = end
            scaled = (end * act.astype(F32)).astype(BF16)
            ss[spans(b), lanes(g)] = scaled
            push[b, g] = dot(ins_t[b], scaled)

        @pl.when((seq == 0) & (seq < seq_n - 1))
        def _():
            advance(g)
            f_copy(g).start()

        return carry

    lax.fori_loop(0, groups, pushed, 0)

    hop = 2
    first = 1

    def work(p):
        pair = pl.ds(pl.multiple_of(p * 128, 128), 128)
        for b in range(blocks):
            scan_p = scan[spans(b), pair]
            grad_p = og_ref[spans(b), pair]
            side = lax.div(iota((BLOCK, 128), 1), width)
            total = jnp.zeros((BLOCK, 128), F32)
            weights = wsum[b]
            for j in range(per):
                h = p * per + j
                scan_h = jnp.where(side == j, scan_p, jnp.zeros_like(scan_p))
                grad_h = jnp.where(side == j, grad_p, jnp.zeros_like(grad_p))
                scores = dot_lanes(scan_h, grad_p)
                column = colb[h, spans(b), :]
                column = jnp.concatenate([column] * (BLOCK // 128), axis=1)
                decay = jnp.exp((rowb[b, h] - column) + mask[b])
                weights = weights + scores * decay
                total = total + dot((inner[b] * decay).astype(BF16), grad_h)
            wsum[b] = weights
            sgrad[spans(b), pair] = total

    def step(k, carry):
        @pl.when(k < pairs)
        def _():
            work(k)

        c_f = k - first - hop * (seq - 1)

        @pl.when((seq > 0) & (c_f >= 0) & (c_f < groups))
        def _():
            f_copy(c_f).wait_recv()

            @pl.when(seq < seq_n - 1)
            def _():
                advance(c_f)
                f_copy(c_f).start()

        c_b = k - hop * (seq_n - 2 - seq)

        @pl.when((seq < seq_n - 1) & (c_b >= 0) & (c_b < groups))
        def _():
            b_copy(c_b).wait_recv()

            @pl.when(seq > 0)
            def _():
                retreat(c_b)
                b_copy(c_b).start()

        return carry

    steps = max(pairs, first + hop * max(seq_n - 2, 0) + groups)
    lax.fori_loop(0, steps, step, 0)

    in_acc = []
    out_acc = []
    for b in range(blocks):
        weights = wsum[b]
        in_acc.append(dot(weights.astype(BF16), co_ref[spans(b), :]))
        out_acc.append(dot(jnp.transpose(weights).astype(BF16), bi_ref[spans(b), :]))
    for c in range(groups):
        part = slice(c * GROUP, (c + 1) * GROUP)
        state = f_in[c]
        for b in range(blocks):
            out_acc[b] = out_acc[b] + dot_lanes(sg[spans(b), part], state)
            if b < blocks - 1:
                state = (whole[b, 0:1, part] * state.astype(F32) + push[b, c]).astype(BF16)
        state = b_in[c]
        for b in reversed(range(blocks)):
            lead[b, c] = state
            in_acc[b] = in_acc[b] + dot_lanes(ss[spans(b), part], state)
            if b > 0:
                state = (whole[b, 0:1, part] * state.astype(F32) + pull[b, c]).astype(BF16)
    for b in range(blocks):
        cbuf[chan, 0, spans(b), :] = in_acc[b].astype(BF16)
        cbuf[chan, 1, spans(b), :] = out_acc[b].astype(BF16)

    def c_copy(step):
        return remote(cbuf.at[chan], cbuf.at[chan], c_send.at[step], c_recv.at[step], peer(step))

    for step_c in range(1, chan_n):
        c_copy(step_c).start()

    def mixed_grads(g, carry):
        rows = [jnp.zeros((1, GROUP), F32)] * taps
        for b in range(blocks):
            cross = dot(bi_ref[spans(b), :], lead[b, g])
            grad = sgrad[spans(b), lanes(g)] + ee[spans(b), lanes(g)] * cross
            rounded = (gs[spans(b), lanes(g)] * grad).astype(BF16)
            if b == 0:
                mg_out[:, lanes(g)] = rounded[:16]
            wide = rounded.astype(F32)
            mgpad[spans(b), lanes(g)] = wide
            for k in range(taps):
                rows[k] = rows[k] + jnp.sum(wide * shifted(b, k, g), axis=0, keepdims=True)
        for k in range(taps):
            wbuf[mine, pl.ds(k, 1), lanes(g)] = rows[k]
        return carry

    lax.fori_loop(0, groups, mixed_grads, 0)

    def m_copy():
        return remote(mg_out, mg_in, m_sem.at[0], m_sem.at[1], {"seq": seq - 1})

    def w_copy(step):
        return remote(wbuf.at[mine], wbuf.at[mine], w_send.at[step], w_recv.at[step], member(step))

    @pl.when(seq > 0)
    def _():
        m_copy().start()

    def w_start(step, carry):
        w_copy(step).start()
        return carry

    lax.fori_loop(1, team, w_start, 0)

    @pl.when(seq == seq_n - 1)
    def _():
        mgpad[pl.ds(local, 8), :] = jnp.zeros((8, channels), F32)

    @pl.when(seq < seq_n - 1)
    def _():
        m_copy().wait_recv()
        mgpad[pl.ds(local, 8), :] = mg_in[...].astype(F32)[:8]

    def input_grads(g, carry):
        for b in range(blocks):
            total = jnp.zeros((BLOCK, GROUP), F32)
            for k in range(taps):
                total = total + w_ref[k : k + 1, lanes(g)] * mgpad[
                    pl.ds(b * BLOCK + taps - 1 - k, BLOCK), lanes(g)
                ]
            ig_ref[spans(b), lanes(g)] = total.astype(BF16)
        return carry

    lax.fori_loop(0, groups, input_grads, 0)

    for step_c in range(1, chan_n):
        c_copy(step_c).wait_recv()
    for index, ref in enumerate((sig_ref, sog_ref)):
        total = cbuf[0, index].astype(F32)
        for source in range(1, chan_n):
            total = total + cbuf[source, index].astype(F32)
        ref[...] = total

    def w_wait(step, carry):
        w_copy(step).wait_recv()
        return carry

    lax.fori_loop(1, team, w_wait, 0)
    total = lax.fori_loop(
        0, team, lambda i, t: t + wbuf[i], jnp.zeros((taps, channels), F32)
    )
    wg_ref[...] = total * (1.0 / math.sqrt(dp_n * seq_n * local))

    def w_left(step, carry):
        w_copy(step).wait_send()
        return carry

    lax.fori_loop(1, team, w_left, 0)
    for step_c in range(1, chan_n):
        c_copy(step_c).wait_send()

    @pl.when(seq < seq_n - 1)
    def _():
        rim_copy().wait_send()
        for c in range(groups):
            f_copy(c).wait_send()

    @pl.when(seq > 0)
    def _():
        m_copy().wait_send()
        for c in range(groups):
            b_copy(c).wait_send()


def per_device(
    sizes, conv_input, conv_weight, log_decay, state_in, state_out, out_grad, lengths, segment_starts
):
    seq_n, chan_n, dp_n = sizes
    batch, local, channels = conv_input.shape
    heads = log_decay.shape[2]
    states = state_in.shape[2]
    taps = conv_weight.shape[0]
    blocks = local // BLOCK
    groups = channels // GROUP
    team = seq_n * dp_n
    vmem = pl.BlockSpec(memory_space=pltpu.VMEM)
    smem = pl.BlockSpec(memory_space=pltpu.SMEM)
    dma = pltpu.SemaphoreType.DMA
    flat = (local, channels)
    states_shape = (groups, states, GROUP)
    outs = pl.pallas_call(
        functools.partial(kernel, seq_n, chan_n, dp_n),
        out_shape=(
            jax.ShapeDtypeStruct(flat, BF16),
            jax.ShapeDtypeStruct((local, states), F32),
            jax.ShapeDtypeStruct((local, states), F32),
            jax.ShapeDtypeStruct((taps, channels), F32),
        ),
        in_specs=[vmem] * 6 + [smem] * 2,
        out_specs=[vmem] * 4,
        scratch_shapes=[
            pltpu.VMEM((16, channels), BF16),
            pltpu.VMEM((local + 8, channels), F32),
            pltpu.VMEM((local + 8, channels), F32),
            pltpu.VMEM(flat, F32),
            pltpu.VMEM(flat, F32),
            pltpu.VMEM(flat, F32),
            pltpu.VMEM((heads, local, 128), F32),
            pltpu.VMEM((blocks, heads, 1, BLOCK), F32),
            pltpu.VMEM((blocks, BLOCK, BLOCK), F32),
            pltpu.VMEM((blocks, BLOCK, BLOCK), F32),
            pltpu.VMEM((blocks, BLOCK, BLOCK), F32),
            pltpu.VMEM((3, local, 2 * heads), BF16),
            pltpu.VMEM((blocks, 8, channels), F32),
            pltpu.VMEM(flat, BF16),
            pltpu.VMEM(flat, BF16),
            pltpu.VMEM(flat, BF16),
            pltpu.VMEM((blocks,) + states_shape, F32),
            pltpu.VMEM((blocks,) + states_shape, F32),
            pltpu.VMEM((blocks,) + states_shape, BF16),
            pltpu.VMEM(states_shape, BF16),
            pltpu.VMEM(states_shape, BF16),
            pltpu.VMEM(states_shape, BF16),
            pltpu.VMEM(states_shape, BF16),
            pltpu.VMEM((chan_n, 2, local, states), BF16),
            pltpu.VMEM((16, channels), BF16),
            pltpu.VMEM((16, channels), BF16),
            pltpu.VMEM((team, taps, channels), F32),
            dma((2,)),
            dma((2, groups)),
            dma((2, groups)),
            dma((2,)),
            dma((chan_n,)),
            dma((chan_n,)),
            dma((team,)),
            dma((team,)),
        ],
        compiler_params=pltpu.CompilerParams(
            collective_id=0, has_side_effects=True, vmem_limit_bytes=56 * 1024 * 1024
        ),
        cost_estimate=pl.CostEstimate(
            flops=4_000_000_000, bytes_accessed=4_000_000, transcendentals=4_000_000
        ),
    )(
        conv_input[0], conv_weight, log_decay[0], state_in[0], state_out[0], out_grad[0],
        lengths, segment_starts,
    )
    return (outs[0][None], outs[1][None], outs[2][None], outs[3])


def solution(mesh):
    sizes = (mesh.shape["seq"], mesh.shape["chan"], mesh.shape["dp"])
    placed = (
        P(("groups", "dp"), "seq", "chan"),
        P(None, "chan"),
        P(("groups", "dp"), "seq", "chan"),
        P(("groups", "dp"), "seq", None),
        P(("groups", "dp"), "seq", None),
        P(("groups", "dp"), "seq", "chan"),
        P(("groups", "dp")),
        P(("groups", "dp"), None),
    )
    return jax.shard_map(
        functools.partial(per_device, sizes),
        mesh=mesh,
        in_specs=placed,
        out_specs=(
            P(("groups", "dp"), "seq", "chan"),
            P(("groups", "dp"), "seq", None),
            P(("groups", "dp"), "seq", None),
            P("groups", "chan"),
        ),
        check_vma=False,
    )
```

```python
import functools
import math

import jax
import jax.numpy as jnp
from jax import lax
from jax.experimental import pallas as pl
from jax.experimental.pallas import tpu as pltpu
from jax.sharding import PartitionSpec as P

BLOCK = 256
GROUP = 256
F32 = jnp.float32
BF16 = jnp.bfloat16
MESH = pl.DeviceIdType.MESH
LANES = (((1,), (1,)), ((), ()))


def dot(a, b):
    return jnp.dot(a, b, preferred_element_type=F32)


def dot_lanes(a, b):
    return lax.dot_general(a, b, LANES, preferred_element_type=F32)


def iota(shape, dim):
    return lax.broadcasted_iota(jnp.int32, shape, dim)


def pack(values):
    upper = values.astype(BF16)
    lower = (values - upper.astype(F32)).astype(BF16)
    return jnp.concatenate([upper, lower], axis=1)


def one_minus_exp(y):
    series = 1.0 / 5040.0
    for term in (720.0, 120.0, 24.0, 6.0, 2.0, 1.0):
        series = series * y + 1.0 / term
    return jnp.where(y > -0.35, -y * series, 1.0 - jnp.exp(y))


def kernel(
    seq_n, chan_n, dp_n,
    x_hbm, w_ref, ld_ref, bi_ref, co_ref, og_hbm, len_ref, st_ref,
    ig_ref, sig_ref, sog_ref, wg_ref,
    x_ref, og_ref, load_sem, rim_in, xpad, mgpad, gs, ee, sgrad, colb, rowb, mask, inner, wsum,
    packs, whole, scan, sg, ss, push, pull, lead,
    f_out, f_in, b_out, b_in, cbuf, mg_out, mg_in, wbuf,
    x_sem, f_sem, b_sem, m_sem, c_send, c_recv, w_send, w_recv,
):
    local, channels = x_hbm.shape
    heads = ld_ref.shape[0]
    width = channels // heads
    taps = w_ref.shape[0]
    blocks = local // BLOCK
    groups = channels // GROUP
    pairs = channels // 128
    per = 128 // width
    starts = st_ref.shape[1]
    team = seq_n * dp_n
    seq = lax.axis_index("seq")
    chan = lax.axis_index("chan")
    core = lax.axis_index("dp")
    mine = seq * dp_n + core

    def member(step):
        other = lax.rem(mine + step, team)
        return {"seq": lax.div(other, dp_n), "dp": lax.rem(other, dp_n)}

    def peer(step):
        return {"chan": lax.rem(chan + step, chan_n)}

    load_x = pltpu.make_async_copy(x_hbm, x_ref, load_sem.at[0])
    load_og = pltpu.make_async_copy(og_hbm, og_ref, load_sem.at[1])
    load_og.start()
    load_x.start()

    barrier = pltpu.get_barrier_semaphore()

    def greet(step, carry):
        pl.semaphore_signal(barrier, inc=1, device_id=member(step), device_id_type=MESH)
        return carry

    lax.fori_loop(1, team, greet, 0)
    for step in range(1, chan_n):
        pl.semaphore_signal(barrier, inc=1, device_id=peer(step), device_id_type=MESH)

    def remote(src, dst, send, recv, target):
        return pltpu.make_async_remote_copy(
            src_ref=src, dst_ref=dst, send_sem=send, recv_sem=recv,
            device_id=target, device_id_type=MESH,
        )

    def spans(b):
        return pl.ds(b * BLOCK, BLOCK)

    length = len_ref[0]
    for b in range(blocks):
        base = seq * local + b * BLOCK
        shape = (BLOCK, heads)
        place = base + iota(shape, 0)
        reset = place == st_ref[0, 0]
        for j in range(1, starts):
            reset = reset | (place == st_ref[0, j])

        def segments(pos):
            total = jnp.zeros(pos.shape, jnp.int32)
            for j in range(starts):
                begin = st_ref[0, j]
                total = total + ((pos >= begin) & (base <= begin)).astype(jnp.int32)
            return total

        segment = segments(place)
        logs = jnp.transpose(ld_ref[:, spans(b)])
        kept = jnp.where(reset, 0.0, logs)
        order_r = iota((BLOCK, BLOCK), 0)
        order_c = iota((BLOCK, BLOCK), 1)
        tri = (order_r >= order_c).astype(F32)
        running = lax.dot_general(
            tri, kept, (((1,), (0,)), ((), ())),
            precision=lax.Precision.HIGHEST, preferred_element_type=F32,
        )
        final = running[BLOCK - 1 :, :]
        start = jnp.where(segment == 0, jnp.exp(running), 0.0)
        end = jnp.where(segment == segment[BLOCK - 1 :, :], jnp.exp(final - running), 0.0)
        valid = place < length
        gain = jnp.where(reset, 1.0, jnp.sqrt(one_minus_exp(2.0 * logs)))
        packs[0, spans(b), :] = pack(jnp.where(valid, start, 0.0))
        packs[1, spans(b), :] = pack(end)
        packs[2, spans(b), :] = pack(jnp.where(valid, gain, 0.0))
        last = jnp.broadcast_to(start[BLOCK - 1 :, :], (16, heads))
        spread_e = (lax.rem(iota((2 * heads, channels), 0), heads)
                    == lax.div(iota((2 * heads, channels), 1), width)).astype(BF16)
        whole[b] = dot(pack(last), spread_e)[:8]
        turned = jnp.transpose(running)
        for h in range(heads):
            colb[h, spans(b), :] = jnp.broadcast_to(running[:, h : h + 1], (BLOCK, 128))
            rowb[b, h] = turned[h : h + 1, :]
        pos_s = base + order_r
        pos_t = base + order_c
        linked = (order_c >= order_r) & (segments(pos_s) == segments(pos_t)) & (pos_t < length)
        mask[b] = jnp.where(linked, 0.0, -jnp.inf)
        inner[b] = dot_lanes(bi_ref[spans(b), :], co_ref[spans(b), :])
        wsum[b] = jnp.zeros((BLOCK, BLOCK), F32)

    def lanes(g):
        return pl.ds(pl.multiple_of(g * GROUP, GROUP), GROUP)

    def spread(g):
        shape = (2 * heads, GROUP)
        head = lax.rem(iota(shape, 0), heads)
        return (head == lax.div(iota(shape, 1) + g * GROUP, width)).astype(BF16)

    pl.semaphore_wait(barrier, team - 1 + chan_n - 1)

    load_og.wait()
    load_x.wait()
    tail = pl.ds(local - 16, 16)

    def rim_copy():
        return remote(x_ref.at[tail], rim_in, x_sem.at[0], x_sem.at[1], {"seq": seq + 1})

    @pl.when(seq < seq_n - 1)
    def _():
        rim_copy().start()

    def f_copy(c):
        return remote(f_out.at[c], f_in.at[c], f_sem.at[0, c], f_sem.at[1, c], {"seq": seq + 1})

    def b_copy(c):
        return remote(b_out.at[c], b_in.at[c], b_sem.at[0, c], b_sem.at[1, c], {"seq": seq - 1})

    def advance(c):
        state = f_in[c].astype(F32)
        for b in range(blocks):
            state = whole[b, 0:1, lanes(c)] * state + push[b, c]
        f_out[c] = state.astype(BF16)

    def retreat(c):
        state = b_in[c].astype(F32)
        for b in reversed(range(blocks)):
            state = whole[b, 0:1, lanes(c)] * state + pull[b, c]
        b_out[c] = state.astype(BF16)

    outs_t = [jnp.transpose(co_ref[spans(b), :].astype(F32)).astype(BF16) for b in range(blocks)]

    @pl.when(seq == seq_n - 1)
    def _():
        b_in[...] = jnp.zeros(b_in.shape, BF16)

    def pulled(g, carry):
        e = spread(g)
        for b in range(blocks):
            scaled = (dot(packs[0, spans(b), :], e) * og_ref[spans(b), lanes(g)].astype(F32)).astype(BF16)
            sg[spans(b), lanes(g)] = scaled
            pull[b, g] = dot(outs_t[b], scaled)

        @pl.when((seq == seq_n - 1) & (seq > 0))
        def _():
            retreat(g)
            b_copy(g).start()

        return carry

    lax.fori_loop(0, groups, pulled, 0)

    xpad[pl.ds(8, local), :] = x_ref[...].astype(F32)

    @pl.when(seq == 0)
    def _():
        xpad[pl.ds(0, 8), :] = jnp.zeros((8, channels), F32)
        f_in[...] = jnp.zeros(f_in.shape, BF16)

    @pl.when(seq > 0)
    def _():
        rim_copy().wait_recv()
        xpad[pl.ds(0, 8), :] = rim_in[...].astype(F32)[8:]

    ins_t = [jnp.transpose(bi_ref[spans(b), :].astype(F32)).astype(BF16) for b in range(blocks)]

    def shifted(b, k, g):
        return xpad[pl.ds(8 + b * BLOCK - (taps - 1) + k, BLOCK), lanes(g)]

    def pushed(g, carry):
        e = spread(g)
        for b in range(blocks):
            mixed = w_ref[0:1, lanes(g)] * shifted(b, 0, g)
            for k in range(1, taps):
                mixed = mixed + w_ref[k : k + 1, lanes(g)] * shifted(b, k, g)
            gate = 0.5 + 0.5 * jnp.tanh(0.5 * mixed)
            gain = dot(packs[2, spans(b), :], e)
            end = dot(packs[1, spans(b), :], e)
            act = (mixed * gate * gain).astype(BF16)
            scan[spans(b), lanes(g)] = act
            gs[spans(b), lanes(g)] = gain * gate * (1.0 + mixed * (1.0 - gate))
            ee[spans(b), lanes(g)] = end
            scaled = (end * act.astype(F32)).astype(BF16)
            ss[spans(b), lanes(g)] = scaled
            push[b, g] = dot(ins_t[b], scaled)

        @pl.when((seq == 0) & (seq < seq_n - 1))
        def _():
            advance(g)
            f_copy(g).start()

        return carry

    lax.fori_loop(0, groups, pushed, 0)

    hop = 2
    first = 1

    def work(p):
        pair = pl.ds(pl.multiple_of(p * 128, 128), 128)
        for b in range(blocks):
            scan_p = scan[spans(b), pair]
            grad_p = og_ref[spans(b), pair]
            side = lax.div(iota((BLOCK, 128), 1), width)
            total = jnp.zeros((BLOCK, 128), F32)
            weights = wsum[b]
            for j in range(per):
                h = p * per + j
                scan_h = jnp.where(side == j, scan_p, jnp.zeros_like(scan_p))
                grad_h = jnp.where(side == j, grad_p, jnp.zeros_like(grad_p))
                scores = dot_lanes(scan_h, grad_p)
                column = colb[h, spans(b), :]
                column = jnp.concatenate([column] * (BLOCK // 128), axis=1)
                decay = jnp.exp((rowb[b, h] - column) + mask[b])
                weights = weights + scores * decay
                total = total + dot((inner[b] * decay).astype(BF16), grad_h)
            wsum[b] = weights
            sgrad[spans(b), pair] = total

    def step(k, carry):
        @pl.when(k < pairs)
        def _():
            work(k)

        c_f = k - first - hop * (seq - 1)

        @pl.when((seq > 0) & (c_f >= 0) & (c_f < groups))
        def _():
            f_copy(c_f).wait_recv()

            @pl.when(seq < seq_n - 1)
            def _():
                advance(c_f)
                f_copy(c_f).start()

        c_b = k - hop * (seq_n - 2 - seq)

        @pl.when((seq < seq_n - 1) & (c_b >= 0) & (c_b < groups))
        def _():
            b_copy(c_b).wait_recv()

            @pl.when(seq > 0)
            def _():
                retreat(c_b)
                b_copy(c_b).start()

        return carry

    steps = max(pairs, first + hop * max(seq_n - 2, 0) + groups)
    lax.fori_loop(0, steps, step, 0)

    in_acc = []
    out_acc = []
    for b in range(blocks):
        weights = wsum[b]
        in_acc.append(dot(weights.astype(BF16), co_ref[spans(b), :]))
        out_acc.append(dot(jnp.transpose(weights).astype(BF16), bi_ref[spans(b), :]))
    for c in range(groups):
        part = slice(c * GROUP, (c + 1) * GROUP)
        state = f_in[c]
        for b in range(blocks):
            out_acc[b] = out_acc[b] + dot_lanes(sg[spans(b), part], state)
            if b < blocks - 1:
                state = (whole[b, 0:1, part] * state.astype(F32) + push[b, c]).astype(BF16)
        state = b_in[c]
        for b in reversed(range(blocks)):
            lead[b, c] = state
            in_acc[b] = in_acc[b] + dot_lanes(ss[spans(b), part], state)
            if b > 0:
                state = (whole[b, 0:1, part] * state.astype(F32) + pull[b, c]).astype(BF16)
    for b in range(blocks):
        cbuf[chan, 0, spans(b), :] = in_acc[b].astype(BF16)
        cbuf[chan, 1, spans(b), :] = out_acc[b].astype(BF16)

    def c_copy(step):
        return remote(cbuf.at[chan], cbuf.at[chan], c_send.at[step], c_recv.at[step], peer(step))

    for step_c in range(1, chan_n):
        c_copy(step_c).start()

    def mixed_grads(g, carry):
        rows = [jnp.zeros((1, GROUP), F32)] * taps
        for b in range(blocks):
            cross = dot(bi_ref[spans(b), :], lead[b, g])
            grad = sgrad[spans(b), lanes(g)] + ee[spans(b), lanes(g)] * cross
            rounded = (gs[spans(b), lanes(g)] * grad).astype(BF16)
            if b == 0:
                mg_out[:, lanes(g)] = rounded[:16]
            wide = rounded.astype(F32)
            mgpad[spans(b), lanes(g)] = wide
            for k in range(taps):
                rows[k] = rows[k] + jnp.sum(wide * shifted(b, k, g), axis=0, keepdims=True)
        for k in range(taps):
            wbuf[mine, pl.ds(k, 1), lanes(g)] = rows[k]
        return carry

    lax.fori_loop(0, groups, mixed_grads, 0)

    def m_copy():
        return remote(mg_out, mg_in, m_sem.at[0], m_sem.at[1], {"seq": seq - 1})

    def w_copy(step):
        return remote(wbuf.at[mine], wbuf.at[mine], w_send.at[step], w_recv.at[step], member(step))

    @pl.when(seq > 0)
    def _():
        m_copy().start()

    def w_start(step, carry):
        w_copy(step).start()
        return carry

    lax.fori_loop(1, team, w_start, 0)

    @pl.when(seq == seq_n - 1)
    def _():
        mgpad[pl.ds(local, 8), :] = jnp.zeros((8, channels), F32)

    @pl.when(seq < seq_n - 1)
    def _():
        m_copy().wait_recv()
        mgpad[pl.ds(local, 8), :] = mg_in[...].astype(F32)[:8]

    def input_grads(g, carry):
        for b in range(blocks):
            total = jnp.zeros((BLOCK, GROUP), F32)
            for k in range(taps):
                total = total + w_ref[k : k + 1, lanes(g)] * mgpad[
                    pl.ds(b * BLOCK + taps - 1 - k, BLOCK), lanes(g)
                ]
            ig_ref[spans(b), lanes(g)] = total.astype(BF16)
        return carry

    lax.fori_loop(0, groups, input_grads, 0)

    for step_c in range(1, chan_n):
        c_copy(step_c).wait_recv()
    for index, ref in enumerate((sig_ref, sog_ref)):
        total = cbuf[0, index].astype(F32)
        for source in range(1, chan_n):
            total = total + cbuf[source, index].astype(F32)
        ref[...] = total

    def w_wait(step, carry):
        w_copy(step).wait_recv()
        return carry

    lax.fori_loop(1, team, w_wait, 0)
    total = lax.fori_loop(
        0, team, lambda i, t: t + wbuf[i], jnp.zeros((taps, channels), F32)
    )
    wg_ref[...] = total * (1.0 / math.sqrt(dp_n * seq_n * local))

    def w_left(step, carry):
        w_copy(step).wait_send()
        return carry

    lax.fori_loop(1, team, w_left, 0)
    for step_c in range(1, chan_n):
        c_copy(step_c).wait_send()

    @pl.when(seq < seq_n - 1)
    def _():
        rim_copy().wait_send()
        for c in range(groups):
            f_copy(c).wait_send()

    @pl.when(seq > 0)
    def _():
        m_copy().wait_send()
        for c in range(groups):
            b_copy(c).wait_send()


def write_out(*refs):
    sems = refs[-1]
    copies = [pltpu.make_async_copy(refs[i], refs[i + 4], sems.at[i]) for i in range(4)]
    for copy in copies:
        copy.start()
    for copy in copies:
        copy.wait()


def per_device(
    sizes, conv_input, conv_weight, log_decay, state_in, state_out, out_grad, lengths, segment_starts
):
    seq_n, chan_n, dp_n = sizes
    batch, local, channels = conv_input.shape
    heads = log_decay.shape[2]
    states = state_in.shape[2]
    taps = conv_weight.shape[0]
    blocks = local // BLOCK
    groups = channels // GROUP
    team = seq_n * dp_n
    vmem = pl.BlockSpec(memory_space=pltpu.VMEM)
    hbm = pl.BlockSpec(memory_space=pltpu.HBM)
    smem = pl.BlockSpec(memory_space=pltpu.SMEM)
    dma = pltpu.SemaphoreType.DMA
    flat = (local, channels)
    states_shape = (groups, states, GROUP)
    outs = pl.pallas_call(
        functools.partial(kernel, seq_n, chan_n, dp_n),
        out_shape=(
            pltpu.VMEM(flat, BF16),
            pltpu.VMEM((local, states), F32),
            pltpu.VMEM((local, states), F32),
            pltpu.VMEM((taps, channels), F32),
        ),
        in_specs=[hbm] + [vmem] * 4 + [hbm] + [smem] * 2,
        out_specs=[vmem] * 4,
        scratch_shapes=[
            pltpu.VMEM(flat, BF16),
            pltpu.VMEM(flat, BF16),
            dma((2,)),
            pltpu.VMEM((16, channels), BF16),
            pltpu.VMEM((local + 8, channels), F32),
            pltpu.VMEM((local + 8, channels), F32),
            pltpu.VMEM(flat, F32),
            pltpu.VMEM(flat, F32),
            pltpu.VMEM(flat, F32),
            pltpu.VMEM((heads, local, 128), F32),
            pltpu.VMEM((blocks, heads, 1, BLOCK), F32),
            pltpu.VMEM((blocks, BLOCK, BLOCK), F32),
            pltpu.VMEM((blocks, BLOCK, BLOCK), F32),
            pltpu.VMEM((blocks, BLOCK, BLOCK), F32),
            pltpu.VMEM((3, local, 2 * heads), BF16),
            pltpu.VMEM((blocks, 8, channels), F32),
            pltpu.VMEM(flat, BF16),
            pltpu.VMEM(flat, BF16),
            pltpu.VMEM(flat, BF16),
            pltpu.VMEM((blocks,) + states_shape, F32),
            pltpu.VMEM((blocks,) + states_shape, F32),
            pltpu.VMEM((blocks,) + states_shape, BF16),
            pltpu.VMEM(states_shape, BF16),
            pltpu.VMEM(states_shape, BF16),
            pltpu.VMEM(states_shape, BF16),
            pltpu.VMEM(states_shape, BF16),
            pltpu.VMEM((chan_n, 2, local, states), BF16),
            pltpu.VMEM((16, channels), BF16),
            pltpu.VMEM((16, channels), BF16),
            pltpu.VMEM((team, taps, channels), F32),
            dma((2,)),
            dma((2, groups)),
            dma((2, groups)),
            dma((2,)),
            dma((chan_n,)),
            dma((chan_n,)),
            dma((team,)),
            dma((team,)),
        ],
        compiler_params=pltpu.CompilerParams(
            collective_id=0, has_side_effects=True, vmem_limit_bytes=61 * 1024 * 1024
        ),
        cost_estimate=pl.CostEstimate(
            flops=4_000_000_000, bytes_accessed=4_000_000, transcendentals=4_000_000
        ),
    )(
        conv_input[0], conv_weight, jnp.transpose(log_decay[0]), state_in[0], state_out[0], out_grad[0],
        lengths, segment_starts,
    )
    outs = pl.pallas_call(
        write_out,
        out_shape=(
            jax.ShapeDtypeStruct(flat, BF16),
            jax.ShapeDtypeStruct((local, states), F32),
            jax.ShapeDtypeStruct((local, states), F32),
            jax.ShapeDtypeStruct((taps, channels), F32),
        ),
        in_specs=[vmem] * 4,
        out_specs=[hbm] * 4,
        scratch_shapes=[dma((4,))],
        compiler_params=pltpu.CompilerParams(vmem_limit_bytes=8 * 1024 * 1024),
    )(*outs)
    return (outs[0][None], outs[1][None], outs[2][None], outs[3])


def solution(mesh):
    sizes = (mesh.shape["seq"], mesh.shape["chan"], mesh.shape["dp"])
    placed = (
        P(("groups", "dp"), "seq", "chan"),
        P(None, "chan"),
        P(("groups", "dp"), "seq", "chan"),
        P(("groups", "dp"), "seq", None),
        P(("groups", "dp"), "seq", None),
        P(("groups", "dp"), "seq", "chan"),
        P(("groups", "dp")),
        P(("groups", "dp"), None),
    )
    return jax.shard_map(
        functools.partial(per_device, sizes),
        mesh=mesh,
        in_specs=placed,
        out_specs=(
            P(("groups", "dp"), "seq", "chan"),
            P(("groups", "dp"), "seq", None),
            P(("groups", "dp"), "seq", None),
            P("groups", "chan"),
        ),
        check_vma=False,
    )
```

```python
import functools
import math

import jax
import jax.numpy as jnp
from jax import lax
from jax.experimental import pallas as pl
from jax.experimental.pallas import tpu as pltpu
from jax.sharding import PartitionSpec as P

BLOCK = 256
GROUP = 128
F32 = jnp.float32
BF16 = jnp.bfloat16
MESH = pl.DeviceIdType.MESH
LANES = (((1,), (1,)), ((), ()))


def dot(a, b):
    return jnp.dot(a, b, preferred_element_type=F32)


def dot_lanes(a, b):
    return lax.dot_general(a, b, LANES, preferred_element_type=F32)


def iota(shape, dim):
    return lax.broadcasted_iota(jnp.int32, shape, dim)


def pack(values):
    upper = values.astype(BF16)
    lower = (values - upper.astype(F32)).astype(BF16)
    return jnp.concatenate([upper, lower], axis=1)


def one_minus_exp(y):
    series = 1.0 / 5040.0
    for term in (720.0, 120.0, 24.0, 6.0, 2.0, 1.0):
        series = series * y + 1.0 / term
    return jnp.where(y > -0.35, -y * series, 1.0 - jnp.exp(y))


def kernel(
    seq_n, chan_n, dp_n,
    x_hbm, w_ref, ld_ref, bi_ref, co_ref, og_hbm, len_ref, st_ref,
    ig_ref, sig_ref, sog_ref, wg_ref,
    x_ref, og_ref, load_sem, rim_in, xpad, mgpad, gs, ee, sgrad, colb, rowb, mask, inner, wsum,
    packs, whole, scan, sg, ss, push, pull, lead,
    f_out, f_in, b_out, b_in, cbuf, mg_out, mg_in, wbuf,
    x_sem, f_sem, b_sem, m_sem, c_send, c_recv, w_send, w_recv,
):
    local, channels = x_hbm.shape
    heads = ld_ref.shape[0]
    width = channels // heads
    taps = w_ref.shape[0]
    blocks = local // BLOCK
    groups = channels // GROUP
    pairs = channels // 128
    per = 128 // width
    starts = st_ref.shape[1]
    team = seq_n * dp_n
    seq = lax.axis_index("seq")
    chan = lax.axis_index("chan")
    core = lax.axis_index("dp")
    mine = seq * dp_n + core

    def member(step):
        other = lax.rem(mine + step, team)
        return {"seq": lax.div(other, dp_n), "dp": lax.rem(other, dp_n)}

    def peer(step):
        return {"chan": lax.rem(chan + step, chan_n)}

    load_x = pltpu.make_async_copy(x_hbm, x_ref, load_sem.at[0])
    load_og = pltpu.make_async_copy(og_hbm, og_ref, load_sem.at[1])
    load_og.start()
    load_x.start()

    barrier = pltpu.get_barrier_semaphore()

    def greet(step, carry):
        pl.semaphore_signal(barrier, inc=1, device_id=member(step), device_id_type=MESH)
        return carry

    lax.fori_loop(1, team, greet, 0)
    for step in range(1, chan_n):
        pl.semaphore_signal(barrier, inc=1, device_id=peer(step), device_id_type=MESH)

    def remote(src, dst, send, recv, target):
        return pltpu.make_async_remote_copy(
            src_ref=src, dst_ref=dst, send_sem=send, recv_sem=recv,
            device_id=target, device_id_type=MESH,
        )

    def spans(b):
        return pl.ds(b * BLOCK, BLOCK)

    length = len_ref[0]
    for b in range(blocks):
        base = seq * local + b * BLOCK
        shape = (BLOCK, heads)
        place = base + iota(shape, 0)
        reset = place == st_ref[0, 0]
        for j in range(1, starts):
            reset = reset | (place == st_ref[0, j])

        def segments(pos):
            total = jnp.zeros(pos.shape, jnp.int32)
            for j in range(starts):
                begin = st_ref[0, j]
                total = total + ((pos >= begin) & (base <= begin)).astype(jnp.int32)
            return total

        segment = segments(place)
        logs = jnp.transpose(ld_ref[:, spans(b)])
        kept = jnp.where(reset, 0.0, logs)
        order_r = iota((BLOCK, BLOCK), 0)
        order_c = iota((BLOCK, BLOCK), 1)
        tri = (order_r >= order_c).astype(F32)
        running = lax.dot_general(
            tri, kept, (((1,), (0,)), ((), ())),
            precision=lax.Precision.HIGHEST, preferred_element_type=F32,
        )
        final = running[BLOCK - 1 :, :]
        start = jnp.where(segment == 0, jnp.exp(running), 0.0)
        end = jnp.where(segment == segment[BLOCK - 1 :, :], jnp.exp(final - running), 0.0)
        valid = place < length
        gain = jnp.where(reset, 1.0, jnp.sqrt(one_minus_exp(2.0 * logs)))
        packs[0, spans(b), :] = pack(jnp.where(valid, start, 0.0))
        packs[1, spans(b), :] = pack(end)
        packs[2, spans(b), :] = pack(jnp.where(valid, gain, 0.0))
        last = jnp.broadcast_to(start[BLOCK - 1 :, :], (16, heads))
        spread_e = (lax.rem(iota((2 * heads, channels), 0), heads)
                    == lax.div(iota((2 * heads, channels), 1), width)).astype(BF16)
        whole[b] = dot(pack(last), spread_e)[:8]
        turned = jnp.transpose(running)
        for h in range(heads):
            colb[h, spans(b), :] = jnp.broadcast_to(running[:, h : h + 1], (BLOCK, 128))
            rowb[b, h] = turned[h : h + 1, :]
        pos_s = base + order_r
        pos_t = base + order_c
        linked = (order_c >= order_r) & (segments(pos_s) == segments(pos_t)) & (pos_t < length)
        mask[b] = jnp.where(linked, 0.0, -jnp.inf)
        inner[b] = dot_lanes(bi_ref[spans(b), :], co_ref[spans(b), :])
        wsum[b] = jnp.zeros((BLOCK, BLOCK), F32)

    def lanes(g):
        return pl.ds(pl.multiple_of(g * GROUP, GROUP), GROUP)

    def spread(g):
        shape = (2 * heads, GROUP)
        head = lax.rem(iota(shape, 0), heads)
        return (head == lax.div(iota(shape, 1) + g * GROUP, width)).astype(BF16)

    pl.semaphore_wait(barrier, team - 1 + chan_n - 1)

    load_og.wait()
    load_x.wait()
    tail = pl.ds(local - 16, 16)

    def rim_copy():
        return remote(x_ref.at[tail], rim_in, x_sem.at[0], x_sem.at[1], {"seq": seq + 1})

    @pl.when(seq < seq_n - 1)
    def _():
        rim_copy().start()

    def f_copy(c):
        return remote(f_out.at[c], f_in.at[c], f_sem.at[0, c], f_sem.at[1, c], {"seq": seq + 1})

    def b_copy(c):
        return remote(b_out.at[c], b_in.at[c], b_sem.at[0, c], b_sem.at[1, c], {"seq": seq - 1})

    def advance(c):
        state = f_in[c].astype(F32)
        for b in range(blocks):
            state = whole[b, 0:1, lanes(c)] * state + push[b, c]
        f_out[c] = state.astype(BF16)

    def retreat(c):
        state = b_in[c].astype(F32)
        for b in reversed(range(blocks)):
            state = whole[b, 0:1, lanes(c)] * state + pull[b, c]
        b_out[c] = state.astype(BF16)

    outs_t = [jnp.transpose(co_ref[spans(b), :].astype(F32)).astype(BF16) for b in range(blocks)]

    @pl.when(seq == seq_n - 1)
    def _():
        b_in[...] = jnp.zeros(b_in.shape, BF16)

    def pulled(g, carry):
        e = spread(g)
        for b in range(blocks):
            scaled = (dot(packs[0, spans(b), :], e) * og_ref[spans(b), lanes(g)].astype(F32)).astype(BF16)
            sg[spans(b), lanes(g)] = scaled
            pull[b, g] = dot(outs_t[b], scaled)

        @pl.when((seq == seq_n - 1) & (seq > 0))
        def _():
            retreat(g)
            b_copy(g).start()

        return carry

    lax.fori_loop(0, groups, pulled, 0)

    xpad[pl.ds(8, local), :] = x_ref[...].astype(F32)

    @pl.when(seq == 0)
    def _():
        xpad[pl.ds(0, 8), :] = jnp.zeros((8, channels), F32)
        f_in[...] = jnp.zeros(f_in.shape, BF16)

    @pl.when(seq > 0)
    def _():
        rim_copy().wait_recv()
        xpad[pl.ds(0, 8), :] = rim_in[...].astype(F32)[8:]

    ins_t = [jnp.transpose(bi_ref[spans(b), :].astype(F32)).astype(BF16) for b in range(blocks)]

    def shifted(b, k, g):
        return xpad[pl.ds(8 + b * BLOCK - (taps - 1) + k, BLOCK), lanes(g)]

    def pushed(g):
        e = spread(g)
        for b in range(blocks):
            mixed = w_ref[0:1, lanes(g)] * shifted(b, 0, g)
            for k in range(1, taps):
                mixed = mixed + w_ref[k : k + 1, lanes(g)] * shifted(b, k, g)
            gate = 0.5 + 0.5 * jnp.tanh(0.5 * mixed)
            gain = dot(packs[2, spans(b), :], e)
            end = dot(packs[1, spans(b), :], e)
            act = (mixed * gate * gain).astype(BF16)
            scan[spans(b), lanes(g)] = act
            gs[spans(b), lanes(g)] = gain * gate * (1.0 + mixed * (1.0 - gate))
            ee[spans(b), lanes(g)] = end
            scaled = (end * act.astype(F32)).astype(BF16)
            ss[spans(b), lanes(g)] = scaled
            push[b, g] = dot(ins_t[b], scaled)

        @pl.when((seq == 0) & (seq < seq_n - 1))
        def _():
            advance(g)
            f_copy(g).start()


    hop = 4

    def work(p):
        pair = pl.ds(pl.multiple_of(p * 128, 128), 128)
        for b in range(blocks):
            scan_p = scan[spans(b), pair]
            grad_p = og_ref[spans(b), pair]
            side = lax.div(iota((BLOCK, 128), 1), width)
            total = jnp.zeros((BLOCK, 128), F32)
            weights = wsum[b]
            for j in range(per):
                h = p * per + j
                scan_h = jnp.where(side == j, scan_p, jnp.zeros_like(scan_p))
                grad_h = jnp.where(side == j, grad_p, jnp.zeros_like(grad_p))
                scores = dot_lanes(scan_h, grad_p)
                column = colb[h, spans(b), :]
                column = jnp.concatenate([column] * (BLOCK // 128), axis=1)
                decay = jnp.exp((rowb[b, h] - column) + mask[b])
                weights = weights + scores * decay
                total = total + dot((inner[b] * decay).astype(BF16), grad_h)
            wsum[b] = weights
            sgrad[spans(b), pair] = total

    def step(k, carry):
        @pl.when(k < groups)
        def _():
            pushed(k)

        @pl.when((k >= groups) & (k < groups + pairs))
        def _():
            work(k - groups)

        c_f = k - hop * seq

        @pl.when((seq > 0) & (seq < seq_n - 1) & (c_f >= 0) & (c_f < groups))
        def _():
            f_copy(c_f).wait_recv()
            advance(c_f)
            f_copy(c_f).start()

        c_b = k - hop * (seq_n - 2 - seq)

        @pl.when((seq > 0) & (seq < seq_n - 1) & (c_b >= 0) & (c_b < groups))
        def _():
            b_copy(c_b).wait_recv()
            retreat(c_b)
            b_copy(c_b).start()

        return carry

    steps = max(groups + pairs, hop * max(seq_n - 2, 0) + groups)
    lax.fori_loop(0, steps, step, 0)

    def c_copy(index, step):
        return remote(
            cbuf.at[chan, index], cbuf.at[chan, index],
            c_send.at[index, step], c_recv.at[index, step], peer(step),
        )

    def out_stage():
        @pl.when(seq == seq_n - 1)
        def _():
            @pl.when(seq > 0)
            def _():
                for c in range(groups):
                    f_copy(c).wait_recv()

        acc = []
        for b in range(blocks):
            acc.append(dot(jnp.transpose(wsum[b]).astype(BF16), bi_ref[spans(b), :]))
        for c in range(groups):
            part = slice(c * GROUP, (c + 1) * GROUP)
            state = f_in[c]
            for b in range(blocks):
                acc[b] = acc[b] + dot_lanes(sg[spans(b), part], state)
                if b < blocks - 1:
                    state = (whole[b, 0:1, part] * state.astype(F32) + push[b, c]).astype(BF16)
        for b in range(blocks):
            cbuf[chan, 1, spans(b), :] = acc[b].astype(BF16)
        for step_c in range(1, chan_n):
            c_copy(1, step_c).start()

    def in_stage():
        @pl.when(seq == 0)
        def _():
            @pl.when(seq < seq_n - 1)
            def _():
                for c in range(groups):
                    b_copy(c).wait_recv()

        acc = []
        for b in range(blocks):
            acc.append(dot(wsum[b].astype(BF16), co_ref[spans(b), :]))
        for c in range(groups):
            part = slice(c * GROUP, (c + 1) * GROUP)
            state = b_in[c]
            for b in reversed(range(blocks)):
                lead[b, c] = state
                acc[b] = acc[b] + dot_lanes(ss[spans(b), part], state)
                if b > 0:
                    state = (whole[b, 0:1, part] * state.astype(F32) + pull[b, c]).astype(BF16)
        for b in range(blocks):
            cbuf[chan, 0, spans(b), :] = acc[b].astype(BF16)
        for step_c in range(1, chan_n):
            c_copy(0, step_c).start()

    early = seq < seq_n // 2

    @pl.when(early)
    def _():
        out_stage()

    in_stage()

    def mixed_grads(b, g, carry):
        cross = dot(bi_ref[spans(b), :], lead[b, g])
        grad = sgrad[spans(b), lanes(g)] + ee[spans(b), lanes(g)] * cross
        rounded = (gs[spans(b), lanes(g)] * grad).astype(BF16)
        if b == 0:
            mg_out[:, lanes(g)] = rounded[:16]
        wide = rounded.astype(F32)
        mgpad[spans(b), lanes(g)] = wide
        for k in range(taps):
            row = jnp.sum(wide * shifted(b, k, g), axis=0, keepdims=True)
            if b > 0:
                row = row + wbuf[mine, pl.ds(k, 1), lanes(g)]
            wbuf[mine, pl.ds(k, 1), lanes(g)] = row
        return carry

    def m_copy():
        return remote(mg_out, mg_in, m_sem.at[0], m_sem.at[1], {"seq": seq - 1})

    def w_copy(step):
        return remote(wbuf.at[mine], wbuf.at[mine], w_send.at[step], w_recv.at[step], member(step))

    lax.fori_loop(0, groups, functools.partial(mixed_grads, 0), 0, unroll=2)

    @pl.when(seq > 0)
    def _():
        m_copy().start()

    for b in range(1, blocks):
        lax.fori_loop(0, groups, functools.partial(mixed_grads, b), 0, unroll=2)

    def w_start(step, carry):
        w_copy(step).start()
        return carry

    lax.fori_loop(1, team, w_start, 0)

    @pl.when(jnp.logical_not(early))
    def _():
        out_stage()

    def input_grads(b, g, carry):
        total = jnp.zeros((BLOCK, GROUP), F32)
        for k in range(taps):
            total = total + w_ref[k : k + 1, lanes(g)] * mgpad[
                pl.ds(b * BLOCK + taps - 1 - k, BLOCK), lanes(g)
            ]
        ig_ref[spans(b), lanes(g)] = total.astype(BF16)
        return carry

    for b in range(blocks):
        if b == blocks - 1:
            @pl.when(seq == seq_n - 1)
            def _():
                mgpad[pl.ds(local, 8), :] = jnp.zeros((8, channels), F32)

            @pl.when(seq < seq_n - 1)
            def _():
                m_copy().wait_recv()
                mgpad[pl.ds(local, 8), :] = mg_in[...].astype(F32)[:8]

        lax.fori_loop(0, groups, functools.partial(input_grads, b), 0, unroll=2)

    for index, ref in enumerate((sig_ref, sog_ref)):
        for step_c in range(1, chan_n):
            c_copy(index, step_c).wait_recv()
        total = cbuf[0, index].astype(F32)
        for source in range(1, chan_n):
            total = total + cbuf[source, index].astype(F32)
        ref[...] = total

    def w_wait(step, carry):
        w_copy(step).wait_recv()
        return carry

    lax.fori_loop(1, team, w_wait, 0)
    total = lax.fori_loop(
        0, team, lambda i, t: t + wbuf[i], jnp.zeros((taps, channels), F32)
    )
    wg_ref[...] = total * (1.0 / math.sqrt(dp_n * seq_n * local))

    def w_left(step, carry):
        w_copy(step).wait_send()
        return carry

    lax.fori_loop(1, team, w_left, 0)
    for index in range(2):
        for step_c in range(1, chan_n):
            c_copy(index, step_c).wait_send()

    @pl.when(seq < seq_n - 1)
    def _():
        rim_copy().wait_send()
        for c in range(groups):
            f_copy(c).wait_send()

    @pl.when(seq > 0)
    def _():
        m_copy().wait_send()
        for c in range(groups):
            b_copy(c).wait_send()


def write_out(*refs):
    sems = refs[-1]
    copies = [pltpu.make_async_copy(refs[i], refs[i + 4], sems.at[i]) for i in range(4)]
    for copy in copies:
        copy.start()
    for copy in copies:
        copy.wait()


def per_device(
    sizes, conv_input, conv_weight, log_decay, state_in, state_out, out_grad, lengths, segment_starts
):
    seq_n, chan_n, dp_n = sizes
    batch, local, channels = conv_input.shape
    heads = log_decay.shape[2]
    states = state_in.shape[2]
    taps = conv_weight.shape[0]
    blocks = local // BLOCK
    groups = channels // GROUP
    team = seq_n * dp_n
    vmem = pl.BlockSpec(memory_space=pltpu.VMEM)
    hbm = pl.BlockSpec(memory_space=pltpu.HBM)
    smem = pl.BlockSpec(memory_space=pltpu.SMEM)
    dma = pltpu.SemaphoreType.DMA
    flat = (local, channels)
    states_shape = (groups, states, GROUP)
    outs = pl.pallas_call(
        functools.partial(kernel, seq_n, chan_n, dp_n),
        out_shape=(
            pltpu.VMEM(flat, BF16),
            pltpu.VMEM((local, states), F32),
            pltpu.VMEM((local, states), F32),
            pltpu.VMEM((taps, channels), F32),
        ),
        in_specs=[hbm] + [vmem] * 4 + [hbm] + [smem] * 2,
        out_specs=[vmem] * 4,
        scratch_shapes=[
            pltpu.VMEM(flat, BF16),
            pltpu.VMEM(flat, BF16),
            dma((2,)),
            pltpu.VMEM((16, channels), BF16),
            pltpu.VMEM((local + 8, channels), F32),
            pltpu.VMEM((local + 8, channels), F32),
            pltpu.VMEM(flat, F32),
            pltpu.VMEM(flat, F32),
            pltpu.VMEM(flat, F32),
            pltpu.VMEM((heads, local, 128), F32),
            pltpu.VMEM((blocks, heads, 1, BLOCK), F32),
            pltpu.VMEM((blocks, BLOCK, BLOCK), F32),
            pltpu.VMEM((blocks, BLOCK, BLOCK), F32),
            pltpu.VMEM((blocks, BLOCK, BLOCK), F32),
            pltpu.VMEM((3, local, 2 * heads), BF16),
            pltpu.VMEM((blocks, 8, channels), F32),
            pltpu.VMEM(flat, BF16),
            pltpu.VMEM(flat, BF16),
            pltpu.VMEM(flat, BF16),
            pltpu.VMEM((blocks,) + states_shape, F32),
            pltpu.VMEM((blocks,) + states_shape, F32),
            pltpu.VMEM((blocks,) + states_shape, BF16),
            pltpu.VMEM(states_shape, BF16),
            pltpu.VMEM(states_shape, BF16),
            pltpu.VMEM(states_shape, BF16),
            pltpu.VMEM(states_shape, BF16),
            pltpu.VMEM((chan_n, 2, local, states), BF16),
            pltpu.VMEM((16, channels), BF16),
            pltpu.VMEM((16, channels), BF16),
            pltpu.VMEM((team, taps, channels), F32),
            dma((2,)),
            dma((2, groups)),
            dma((2, groups)),
            dma((2,)),
            dma((2, chan_n)),
            dma((2, chan_n)),
            dma((team,)),
            dma((team,)),
        ],
        compiler_params=pltpu.CompilerParams(
            collective_id=0, has_side_effects=True, vmem_limit_bytes=61 * 1024 * 1024
        ),
        cost_estimate=pl.CostEstimate(
            flops=4_000_000_000, bytes_accessed=4_000_000, transcendentals=4_000_000
        ),
    )(
        conv_input[0], conv_weight, jnp.transpose(log_decay[0]), state_in[0], state_out[0], out_grad[0],
        lengths, segment_starts,
    )
    outs = pl.pallas_call(
        write_out,
        out_shape=(
            jax.ShapeDtypeStruct(flat, BF16),
            jax.ShapeDtypeStruct((local, states), F32),
            jax.ShapeDtypeStruct((local, states), F32),
            jax.ShapeDtypeStruct((taps, channels), F32),
        ),
        in_specs=[vmem] * 4,
        out_specs=[hbm] * 4,
        scratch_shapes=[dma((4,))],
        compiler_params=pltpu.CompilerParams(vmem_limit_bytes=8 * 1024 * 1024),
    )(*outs)
    return (outs[0][None], outs[1][None], outs[2][None], outs[3])


def solution(mesh):
    sizes = (mesh.shape["seq"], mesh.shape["chan"], mesh.shape["dp"])
    placed = (
        P(("groups", "dp"), "seq", "chan"),
        P(None, "chan"),
        P(("groups", "dp"), "seq", "chan"),
        P(("groups", "dp"), "seq", None),
        P(("groups", "dp"), "seq", None),
        P(("groups", "dp"), "seq", "chan"),
        P(("groups", "dp")),
        P(("groups", "dp"), None),
    )
    return jax.shard_map(
        functools.partial(per_device, sizes),
        mesh=mesh,
        in_specs=placed,
        out_specs=(
            P(("groups", "dp"), "seq", "chan"),
            P(("groups", "dp"), "seq", None),
            P(("groups", "dp"), "seq", None),
            P("groups", "chan"),
        ),
        check_vma=False,
    )
```

```python
import functools
import math

import jax
import jax.numpy as jnp
from jax import lax
from jax.experimental import pallas as pl
from jax.experimental.pallas import tpu as pltpu
from jax.sharding import PartitionSpec as P

BLOCK = 256
GROUP = 256
F32 = jnp.float32
BF16 = jnp.bfloat16
MESH = pl.DeviceIdType.MESH
LANES = (((1,), (1,)), ((), ()))


def dot(a, b):
    return jnp.dot(a, b, preferred_element_type=F32)


def dot_lanes(a, b):
    return lax.dot_general(a, b, LANES, preferred_element_type=F32)


def iota(shape, dim):
    return lax.broadcasted_iota(jnp.int32, shape, dim)


def pack(values):
    upper = values.astype(BF16)
    lower = (values - upper.astype(F32)).astype(BF16)
    return jnp.concatenate([upper, lower], axis=1)


def one_minus_exp(y):
    series = 1.0 / 5040.0
    for term in (720.0, 120.0, 24.0, 6.0, 2.0, 1.0):
        series = series * y + 1.0 / term
    return jnp.where(y > -0.35, -y * series, 1.0 - jnp.exp(y))


def kernel(
    seq_n, chan_n, dp_n,
    x_hbm, w_ref, ld_ref, bi_ref, co_ref, og_hbm, len_ref, st_ref,
    ig_ref, sig_ref, sog_ref, wg_ref,
    x_ref, og_ref, load_sem, rim_in, xpad, mgpad, gs, ee, sgrad, colb, rowb, mask, inner, wsum,
    packs, whole, scan, sg, ss, push, pull, lead,
    f_out, f_in, b_out, b_in, cbuf, mg_out, mg_in, wbuf,
    x_sem, f_sem, b_sem, m_sem, c_send, c_recv, w_send, w_recv,
):
    local, channels = x_hbm.shape
    heads = ld_ref.shape[0]
    width = channels // heads
    taps = w_ref.shape[0]
    blocks = local // BLOCK
    groups = channels // GROUP
    pairs = channels // 128
    per = 128 // width
    starts = st_ref.shape[1]
    team = seq_n * dp_n
    seq = lax.axis_index("seq")
    chan = lax.axis_index("chan")
    core = lax.axis_index("dp")
    mine = seq * dp_n + core

    def member(step):
        other = lax.rem(mine + step, team)
        return {"seq": lax.div(other, dp_n), "dp": lax.rem(other, dp_n)}

    def peer(step):
        return {"chan": lax.rem(chan + step, chan_n)}

    load_x = pltpu.make_async_copy(x_hbm, x_ref, load_sem.at[0])
    load_og = pltpu.make_async_copy(og_hbm, og_ref, load_sem.at[1])
    load_og.start()
    load_x.start()

    barrier = pltpu.get_barrier_semaphore()

    def greet(step, carry):
        pl.semaphore_signal(barrier, inc=1, device_id=member(step), device_id_type=MESH)
        return carry

    lax.fori_loop(1, team, greet, 0)
    for step in range(1, chan_n):
        pl.semaphore_signal(barrier, inc=1, device_id=peer(step), device_id_type=MESH)

    def remote(src, dst, send, recv, target):
        return pltpu.make_async_remote_copy(
            src_ref=src, dst_ref=dst, send_sem=send, recv_sem=recv,
            device_id=target, device_id_type=MESH,
        )

    def spans(b):
        return pl.ds(b * BLOCK, BLOCK)

    length = len_ref[0]
    for b in range(blocks):
        base = seq * local + b * BLOCK
        shape = (BLOCK, heads)
        place = base + iota(shape, 0)
        reset = place == st_ref[0, 0]
        for j in range(1, starts):
            reset = reset | (place == st_ref[0, j])

        def segments(pos):
            total = jnp.zeros(pos.shape, jnp.int32)
            for j in range(starts):
                begin = st_ref[0, j]
                total = total + ((pos >= begin) & (base <= begin)).astype(jnp.int32)
            return total

        segment = segments(place)
        logs = jnp.transpose(ld_ref[:, spans(b)])
        kept = jnp.where(reset, 0.0, logs)
        order_r = iota((BLOCK, BLOCK), 0)
        order_c = iota((BLOCK, BLOCK), 1)
        tri = (order_r >= order_c).astype(F32)
        running = lax.dot_general(
            tri, kept, (((1,), (0,)), ((), ())),
            precision=lax.Precision.HIGHEST, preferred_element_type=F32,
        )
        final = running[BLOCK - 1 :, :]
        start = jnp.where(segment == 0, jnp.exp(running), 0.0)
        end = jnp.where(segment == segment[BLOCK - 1 :, :], jnp.exp(final - running), 0.0)
        valid = place < length
        gain = jnp.where(reset, 1.0, jnp.sqrt(one_minus_exp(2.0 * logs)))
        packs[0, spans(b), :] = pack(jnp.where(valid, start, 0.0))
        packs[1, spans(b), :] = pack(end)
        packs[2, spans(b), :] = pack(jnp.where(valid, gain, 0.0))
        last = jnp.broadcast_to(start[BLOCK - 1 :, :], (16, heads))
        spread_e = (lax.rem(iota((2 * heads, channels), 0), heads)
                    == lax.div(iota((2 * heads, channels), 1), width)).astype(BF16)
        whole[b] = dot(pack(last), spread_e)[:8]
        turned = jnp.transpose(running)
        for h in range(heads):
            colb[h, spans(b), :] = jnp.broadcast_to(running[:, h : h + 1], (BLOCK, 128))
            rowb[b, h] = turned[h : h + 1, :]
        pos_s = base + order_r
        pos_t = base + order_c
        linked = (order_c >= order_r) & (segments(pos_s) == segments(pos_t)) & (pos_t < length)
        mask[b] = jnp.where(linked, 0.0, -jnp.inf)
        inner[b] = dot_lanes(bi_ref[spans(b), :], co_ref[spans(b), :])
        wsum[b] = jnp.zeros((BLOCK, BLOCK), F32)

    def lanes(g):
        return pl.ds(pl.multiple_of(g * GROUP, GROUP), GROUP)

    def spread(g):
        shape = (2 * heads, GROUP)
        head = lax.rem(iota(shape, 0), heads)
        return (head == lax.div(iota(shape, 1) + g * GROUP, width)).astype(BF16)

    pl.semaphore_wait(barrier, team - 1 + chan_n - 1)

    load_og.wait()
    load_x.wait()
    tail = pl.ds(local - 16, 16)

    def rim_copy():
        return remote(x_ref.at[tail], rim_in, x_sem.at[0], x_sem.at[1], {"seq": seq + 1})

    @pl.when(seq < seq_n - 1)
    def _():
        rim_copy().start()

    def f_copy(c):
        return remote(f_out.at[c], f_in.at[c], f_sem.at[0, c], f_sem.at[1, c], {"seq": seq + 1})

    def b_copy(c):
        return remote(b_out.at[c], b_in.at[c], b_sem.at[0, c], b_sem.at[1, c], {"seq": seq - 1})

    def advance(c):
        state = f_in[c].astype(F32)
        for b in range(blocks):
            state = whole[b, 0:1, lanes(c)] * state + push[b, c]
        f_out[c] = state.astype(BF16)

    def retreat(c):
        state = b_in[c].astype(F32)
        for b in reversed(range(blocks)):
            state = whole[b, 0:1, lanes(c)] * state + pull[b, c]
        b_out[c] = state.astype(BF16)

    outs_t = [jnp.transpose(co_ref[spans(b), :].astype(F32)).astype(BF16) for b in range(blocks)]

    @pl.when(seq == seq_n - 1)
    def _():
        b_in[...] = jnp.zeros(b_in.shape, BF16)

    def pulled(g, carry):
        e = spread(g)
        for b in range(blocks):
            scaled = (dot(packs[0, spans(b), :], e) * og_ref[spans(b), lanes(g)].astype(F32)).astype(BF16)
            sg[spans(b), lanes(g)] = scaled
            pull[b, g] = dot(outs_t[b], scaled)

        @pl.when((seq == seq_n - 1) & (seq > 0))
        def _():
            retreat(g)
            b_copy(g).start()

        return carry

    lax.fori_loop(0, groups, pulled, 0)

    xpad[pl.ds(8, local), :] = x_ref[...].astype(F32)

    @pl.when(seq == 0)
    def _():
        xpad[pl.ds(0, 8), :] = jnp.zeros((8, channels), F32)
        f_in[...] = jnp.zeros(f_in.shape, BF16)

    @pl.when(seq > 0)
    def _():
        rim_copy().wait_recv()
        xpad[pl.ds(0, 8), :] = rim_in[...].astype(F32)[8:]

    ins_t = [jnp.transpose(bi_ref[spans(b), :].astype(F32)).astype(BF16) for b in range(blocks)]

    def shifted(b, k, g):
        return xpad[pl.ds(8 + b * BLOCK - (taps - 1) + k, BLOCK), lanes(g)]

    def pushed(g):
        e = spread(g)
        for b in range(blocks):
            mixed = w_ref[0:1, lanes(g)] * shifted(b, 0, g)
            for k in range(1, taps):
                mixed = mixed + w_ref[k : k + 1, lanes(g)] * shifted(b, k, g)
            gate = 0.5 + 0.5 * jnp.tanh(0.5 * mixed)
            gain = dot(packs[2, spans(b), :], e)
            end = dot(packs[1, spans(b), :], e)
            act = (mixed * gate * gain).astype(BF16)
            scan[spans(b), lanes(g)] = act
            gs[spans(b), lanes(g)] = gain * gate * (1.0 + mixed * (1.0 - gate))
            ee[spans(b), lanes(g)] = end
            scaled = (end * act.astype(F32)).astype(BF16)
            ss[spans(b), lanes(g)] = scaled
            push[b, g] = dot(ins_t[b], scaled)

        @pl.when((seq == 0) & (seq < seq_n - 1))
        def _():
            advance(g)
            f_copy(g).start()


    hop = 4

    def work(p):
        pair = pl.ds(pl.multiple_of(p * 128, 128), 128)
        for b in range(blocks):
            scan_p = scan[spans(b), pair]
            grad_p = og_ref[spans(b), pair]
            side = lax.div(iota((BLOCK, 128), 1), width)
            total = jnp.zeros((BLOCK, 128), F32)
            weights = wsum[b]
            for j in range(per):
                h = p * per + j
                scan_h = jnp.where(side == j, scan_p, jnp.zeros_like(scan_p))
                grad_h = jnp.where(side == j, grad_p, jnp.zeros_like(grad_p))
                scores = dot_lanes(scan_h, grad_p)
                column = colb[h, spans(b), :]
                column = jnp.concatenate([column] * (BLOCK // 128), axis=1)
                decay = jnp.exp((rowb[b, h] - column) + mask[b])
                weights = weights + scores * decay
                total = total + dot((inner[b] * decay).astype(BF16), grad_h)
            wsum[b] = weights
            sgrad[spans(b), pair] = total

    def step(k, carry):
        @pl.when(k < groups)
        def _():
            pushed(k)

        @pl.when((k >= groups) & (k < groups + pairs))
        def _():
            work(k - groups)

        c_f = k - hop * seq

        @pl.when((seq > 0) & (seq < seq_n - 1) & (c_f >= 0) & (c_f < groups))
        def _():
            f_copy(c_f).wait_recv()
            advance(c_f)
            f_copy(c_f).start()

        c_b = k - hop * (seq_n - 2 - seq)

        @pl.when((seq > 0) & (seq < seq_n - 1) & (c_b >= 0) & (c_b < groups))
        def _():
            b_copy(c_b).wait_recv()
            retreat(c_b)
            b_copy(c_b).start()

        return carry

    steps = max(groups + pairs, hop * max(seq_n - 2, 0) + groups)
    lax.fori_loop(0, steps, step, 0)

    def c_copy(index, step):
        return remote(
            cbuf.at[chan, index], cbuf.at[chan, index],
            c_send.at[index, step], c_recv.at[index, step], peer(step),
        )

    def out_stage():
        @pl.when(seq == seq_n - 1)
        def _():
            @pl.when(seq > 0)
            def _():
                for c in range(groups):
                    f_copy(c).wait_recv()

        acc = []
        for b in range(blocks):
            acc.append(dot(jnp.transpose(wsum[b]).astype(BF16), bi_ref[spans(b), :]))
        for c in range(groups):
            part = slice(c * GROUP, (c + 1) * GROUP)
            state = f_in[c]
            for b in range(blocks):
                acc[b] = acc[b] + dot_lanes(sg[spans(b), part], state)
                if b < blocks - 1:
                    state = (whole[b, 0:1, part] * state.astype(F32) + push[b, c]).astype(BF16)
        for b in range(blocks):
            cbuf[chan, 1, spans(b), :] = acc[b].astype(BF16)
        for step_c in range(1, chan_n):
            c_copy(1, step_c).start()

    def in_stage():
        @pl.when(seq == 0)
        def _():
            @pl.when(seq < seq_n - 1)
            def _():
                for c in range(groups):
                    b_copy(c).wait_recv()

        acc = []
        for b in range(blocks):
            acc.append(dot(wsum[b].astype(BF16), co_ref[spans(b), :]))
        for c in range(groups):
            part = slice(c * GROUP, (c + 1) * GROUP)
            state = b_in[c]
            for b in reversed(range(blocks)):
                lead[b, c] = state
                acc[b] = acc[b] + dot_lanes(ss[spans(b), part], state)
                if b > 0:
                    state = (whole[b, 0:1, part] * state.astype(F32) + pull[b, c]).astype(BF16)
        for b in range(blocks):
            cbuf[chan, 0, spans(b), :] = acc[b].astype(BF16)
        for step_c in range(1, chan_n):
            c_copy(0, step_c).start()

    early = seq < seq_n // 2

    @pl.when(early)
    def _():
        out_stage()

    in_stage()

    def mixed_grads(b, g, carry):
        cross = dot(bi_ref[spans(b), :], lead[b, g])
        grad = sgrad[spans(b), lanes(g)] + ee[spans(b), lanes(g)] * cross
        rounded = (gs[spans(b), lanes(g)] * grad).astype(BF16)
        if b == 0:
            mg_out[:, lanes(g)] = rounded[:16]
        wide = rounded.astype(F32)
        mgpad[spans(b), lanes(g)] = wide
        for k in range(taps):
            row = jnp.sum(wide * shifted(b, k, g), axis=0, keepdims=True)
            if b > 0:
                row = row + wbuf[mine, pl.ds(k, 1), lanes(g)]
            wbuf[mine, pl.ds(k, 1), lanes(g)] = row
        return carry

    def m_copy():
        return remote(mg_out, mg_in, m_sem.at[0], m_sem.at[1], {"seq": seq - 1})

    def w_copy(step):
        return remote(wbuf.at[mine], wbuf.at[mine], w_send.at[step], w_recv.at[step], member(step))

    lax.fori_loop(0, groups, functools.partial(mixed_grads, 0), 0, unroll=4)

    @pl.when(seq > 0)
    def _():
        m_copy().start()

    for b in range(1, blocks):
        lax.fori_loop(0, groups, functools.partial(mixed_grads, b), 0, unroll=4)

    def w_start(step, carry):
        w_copy(step).start()
        return carry

    lax.fori_loop(1, team, w_start, 0)

    @pl.when(jnp.logical_not(early))
    def _():
        out_stage()

    def input_grads(b, g, carry):
        total = jnp.zeros((BLOCK, GROUP), F32)
        for k in range(taps):
            total = total + w_ref[k : k + 1, lanes(g)] * mgpad[
                pl.ds(b * BLOCK + taps - 1 - k, BLOCK), lanes(g)
            ]
        ig_ref[spans(b), lanes(g)] = total.astype(BF16)
        return carry

    for b in range(blocks):
        if b == blocks - 1:
            @pl.when(seq == seq_n - 1)
            def _():
                mgpad[pl.ds(local, 8), :] = jnp.zeros((8, channels), F32)

            @pl.when(seq < seq_n - 1)
            def _():
                m_copy().wait_recv()
                mgpad[pl.ds(local, 8), :] = mg_in[...].astype(F32)[:8]

        lax.fori_loop(0, groups, functools.partial(input_grads, b), 0, unroll=4)

    for index, ref in enumerate((sig_ref, sog_ref)):
        for step_c in range(1, chan_n):
            c_copy(index, step_c).wait_recv()
        total = cbuf[0, index].astype(F32)
        for source in range(1, chan_n):
            total = total + cbuf[source, index].astype(F32)
        ref[...] = total

    def w_wait(step, carry):
        w_copy(step).wait_recv()
        return carry

    lax.fori_loop(1, team, w_wait, 0)
    total = lax.fori_loop(
        0, team, lambda i, t: t + wbuf[i], jnp.zeros((taps, channels), F32)
    )
    wg_ref[...] = total * (1.0 / math.sqrt(dp_n * seq_n * local))

    def w_left(step, carry):
        w_copy(step).wait_send()
        return carry

    lax.fori_loop(1, team, w_left, 0)
    for index in range(2):
        for step_c in range(1, chan_n):
            c_copy(index, step_c).wait_send()

    @pl.when(seq < seq_n - 1)
    def _():
        rim_copy().wait_send()
        for c in range(groups):
            f_copy(c).wait_send()

    @pl.when(seq > 0)
    def _():
        m_copy().wait_send()
        for c in range(groups):
            b_copy(c).wait_send()


def write_out(*refs):
    sems = refs[-1]
    copies = [pltpu.make_async_copy(refs[i], refs[i + 4], sems.at[i]) for i in range(4)]
    for copy in copies:
        copy.start()
    for copy in copies:
        copy.wait()


def per_device(
    sizes, conv_input, conv_weight, log_decay, state_in, state_out, out_grad, lengths, segment_starts
):
    seq_n, chan_n, dp_n = sizes
    batch, local, channels = conv_input.shape
    heads = log_decay.shape[2]
    states = state_in.shape[2]
    taps = conv_weight.shape[0]
    blocks = local // BLOCK
    groups = channels // GROUP
    team = seq_n * dp_n
    vmem = pl.BlockSpec(memory_space=pltpu.VMEM)
    hbm = pl.BlockSpec(memory_space=pltpu.HBM)
    smem = pl.BlockSpec(memory_space=pltpu.SMEM)
    dma = pltpu.SemaphoreType.DMA
    flat = (local, channels)
    states_shape = (groups, states, GROUP)
    outs = pl.pallas_call(
        functools.partial(kernel, seq_n, chan_n, dp_n),
        out_shape=(
            pltpu.VMEM(flat, BF16),
            pltpu.VMEM((local, states), F32),
            pltpu.VMEM((local, states), F32),
            pltpu.VMEM((taps, channels), F32),
        ),
        in_specs=[hbm] + [vmem] * 4 + [hbm] + [smem] * 2,
        out_specs=[vmem] * 4,
        scratch_shapes=[
            pltpu.VMEM(flat, BF16),
            pltpu.VMEM(flat, BF16),
            dma((2,)),
            pltpu.VMEM((16, channels), BF16),
            pltpu.VMEM((local + 8, channels), F32),
            pltpu.VMEM((local + 8, channels), F32),
            pltpu.VMEM(flat, F32),
            pltpu.VMEM(flat, F32),
            pltpu.VMEM(flat, F32),
            pltpu.VMEM((heads, local, 128), F32),
            pltpu.VMEM((blocks, heads, 1, BLOCK), F32),
            pltpu.VMEM((blocks, BLOCK, BLOCK), F32),
            pltpu.VMEM((blocks, BLOCK, BLOCK), F32),
            pltpu.VMEM((blocks, BLOCK, BLOCK), F32),
            pltpu.VMEM((3, local, 2 * heads), BF16),
            pltpu.VMEM((blocks, 8, channels), F32),
            pltpu.VMEM(flat, BF16),
            pltpu.VMEM(flat, BF16),
            pltpu.VMEM(flat, BF16),
            pltpu.VMEM((blocks,) + states_shape, F32),
            pltpu.VMEM((blocks,) + states_shape, F32),
            pltpu.VMEM((blocks,) + states_shape, BF16),
            pltpu.VMEM(states_shape, BF16),
            pltpu.VMEM(states_shape, BF16),
            pltpu.VMEM(states_shape, BF16),
            pltpu.VMEM(states_shape, BF16),
            pltpu.VMEM((chan_n, 2, local, states), BF16),
            pltpu.VMEM((16, channels), BF16),
            pltpu.VMEM((16, channels), BF16),
            pltpu.VMEM((team, taps, channels), F32),
            dma((2,)),
            dma((2, groups)),
            dma((2, groups)),
            dma((2,)),
            dma((2, chan_n)),
            dma((2, chan_n)),
            dma((team,)),
            dma((team,)),
        ],
        compiler_params=pltpu.CompilerParams(
            collective_id=0, has_side_effects=True, vmem_limit_bytes=61 * 1024 * 1024
        ),
        cost_estimate=pl.CostEstimate(
            flops=4_000_000_000, bytes_accessed=4_000_000, transcendentals=4_000_000
        ),
    )(
        conv_input[0], conv_weight, jnp.transpose(log_decay[0]), state_in[0], state_out[0], out_grad[0],
        lengths, segment_starts,
    )
    outs = pl.pallas_call(
        write_out,
        out_shape=(
            jax.ShapeDtypeStruct(flat, BF16),
            jax.ShapeDtypeStruct((local, states), F32),
            jax.ShapeDtypeStruct((local, states), F32),
            jax.ShapeDtypeStruct((taps, channels), F32),
        ),
        in_specs=[vmem] * 4,
        out_specs=[hbm] * 4,
        scratch_shapes=[dma((4,))],
        compiler_params=pltpu.CompilerParams(vmem_limit_bytes=8 * 1024 * 1024),
    )(*outs)
    return (outs[0][None], outs[1][None], outs[2][None], outs[3])


def solution(mesh):
    sizes = (mesh.shape["seq"], mesh.shape["chan"], mesh.shape["dp"])
    placed = (
        P(("groups", "dp"), "seq", "chan"),
        P(None, "chan"),
        P(("groups", "dp"), "seq", "chan"),
        P(("groups", "dp"), "seq", None),
        P(("groups", "dp"), "seq", None),
        P(("groups", "dp"), "seq", "chan"),
        P(("groups", "dp")),
        P(("groups", "dp"), None),
    )
    return jax.shard_map(
        functools.partial(per_device, sizes),
        mesh=mesh,
        in_specs=placed,
        out_specs=(
            P(("groups", "dp"), "seq", "chan"),
            P(("groups", "dp"), "seq", None),
            P(("groups", "dp"), "seq", None),
            P("groups", "chan"),
        ),
        check_vma=False,
    )
```

```python
import functools
import math

import jax
import jax.numpy as jnp
from jax import lax
from jax.experimental import pallas as pl
from jax.experimental.pallas import tpu as pltpu
from jax.sharding import PartitionSpec as P

BLOCK = 256
GROUP = 256
F32 = jnp.float32
BF16 = jnp.bfloat16
MESH = pl.DeviceIdType.MESH
LANES = (((1,), (1,)), ((), ()))


def dot(a, b):
    return jnp.dot(a, b, preferred_element_type=F32)


def dot_lanes(a, b):
    return lax.dot_general(a, b, LANES, preferred_element_type=F32)


def iota(shape, dim):
    return lax.broadcasted_iota(jnp.int32, shape, dim)


def pack(values):
    upper = values.astype(BF16)
    lower = (values - upper.astype(F32)).astype(BF16)
    return jnp.concatenate([upper, lower], axis=1)


def one_minus_exp(y):
    series = 1.0 / 5040.0
    for term in (720.0, 120.0, 24.0, 6.0, 2.0, 1.0):
        series = series * y + 1.0 / term
    return jnp.where(y > -0.35, -y * series, 1.0 - jnp.exp(y))


def kernel(
    seq_n, chan_n, dp_n,
    x_hbm, w_ref, ld_ref, bi_ref, co_ref, og_hbm, len_ref, st_ref,
    ig_ref, sig_ref, sog_ref, wg_ref,
    x_ref, og_ref, load_sem, rim_in, xpad, mgpad, gs, ee, sgrad, colb, rowb, mask, inner, wsum,
    packs, whole, scan, sg, ss, push, pull, lead,
    f_out, f_in, b_out, b_in, cbuf, mg_out, mg_in, wbuf,
    x_sem, f_sem, b_sem, m_sem, c_send, c_recv, w_send, w_recv,
):
    local, channels = x_hbm.shape
    heads = ld_ref.shape[0]
    width = channels // heads
    taps = w_ref.shape[0]
    blocks = local // BLOCK
    groups = channels // GROUP
    pairs = channels // 128
    per = 128 // width
    starts = st_ref.shape[1]
    team = seq_n * dp_n
    seq = lax.axis_index("seq")
    chan = lax.axis_index("chan")
    core = lax.axis_index("dp")
    mine = seq * dp_n + core

    def member(step):
        other = lax.rem(mine + step, team)
        return {"seq": lax.div(other, dp_n), "dp": lax.rem(other, dp_n)}

    def peer(step):
        return {"chan": lax.rem(chan + step, chan_n)}

    load_x = pltpu.make_async_copy(x_hbm, x_ref, load_sem.at[0])
    load_og = pltpu.make_async_copy(og_hbm, og_ref, load_sem.at[1])
    load_og.start()
    load_x.start()

    barrier = pltpu.get_barrier_semaphore()

    def greet(step, carry):
        pl.semaphore_signal(barrier, inc=1, device_id=member(step), device_id_type=MESH)
        return carry

    lax.fori_loop(1, team, greet, 0)
    for step in range(1, chan_n):
        pl.semaphore_signal(barrier, inc=1, device_id=peer(step), device_id_type=MESH)

    def remote(src, dst, send, recv, target):
        return pltpu.make_async_remote_copy(
            src_ref=src, dst_ref=dst, send_sem=send, recv_sem=recv,
            device_id=target, device_id_type=MESH,
        )

    def spans(b):
        return pl.ds(b * BLOCK, BLOCK)

    length = len_ref[0]
    for b in range(blocks):
        base = seq * local + b * BLOCK
        shape = (BLOCK, heads)
        place = base + iota(shape, 0)
        reset = place == st_ref[0, 0]
        for j in range(1, starts):
            reset = reset | (place == st_ref[0, j])

        def segments(pos):
            total = jnp.zeros(pos.shape, jnp.int32)
            for j in range(starts):
                begin = st_ref[0, j]
                total = total + ((pos >= begin) & (base <= begin)).astype(jnp.int32)
            return total

        segment = segments(place)
        logs = jnp.transpose(ld_ref[:, spans(b)])
        kept = jnp.where(reset, 0.0, logs)
        order_r = iota((BLOCK, BLOCK), 0)
        order_c = iota((BLOCK, BLOCK), 1)
        tri = (order_r >= order_c).astype(F32)
        running = lax.dot_general(
            tri, kept, (((1,), (0,)), ((), ())),
            precision=lax.Precision.HIGHEST, preferred_element_type=F32,
        )
        final = running[BLOCK - 1 :, :]
        start = jnp.where(segment == 0, jnp.exp(running), 0.0)
        end = jnp.where(segment == segment[BLOCK - 1 :, :], jnp.exp(final - running), 0.0)
        valid = place < length
        gain = jnp.where(reset, 1.0, jnp.sqrt(one_minus_exp(2.0 * logs)))
        packs[0, spans(b), :] = pack(jnp.where(valid, start, 0.0))
        packs[1, spans(b), :] = pack(end)
        packs[2, spans(b), :] = pack(jnp.where(valid, gain, 0.0))
        last = jnp.broadcast_to(start[BLOCK - 1 :, :], (16, heads))
        spread_e = (lax.rem(iota((2 * heads, channels), 0), heads)
                    == lax.div(iota((2 * heads, channels), 1), width)).astype(BF16)
        whole[b] = dot(pack(last), spread_e)[:8]
        turned = jnp.transpose(running)
        for h in range(heads):
            colb[h, spans(b), :] = jnp.broadcast_to(running[:, h : h + 1], (BLOCK, 128))
            rowb[b, h] = turned[h : h + 1, :]
        pos_s = base + order_r
        pos_t = base + order_c
        linked = (order_c >= order_r) & (segments(pos_s) == segments(pos_t)) & (pos_t < length)
        mask[b] = jnp.where(linked, 0.0, -jnp.inf)
        inner[b] = dot_lanes(bi_ref[spans(b), :], co_ref[spans(b), :])
        wsum[b] = jnp.zeros((BLOCK, BLOCK), F32)

    def lanes(g):
        return pl.ds(pl.multiple_of(g * GROUP, GROUP), GROUP)

    def spread(g):
        shape = (2 * heads, GROUP)
        head = lax.rem(iota(shape, 0), heads)
        return (head == lax.div(iota(shape, 1) + g * GROUP, width)).astype(BF16)

    pl.semaphore_wait(barrier, team - 1 + chan_n - 1)

    load_og.wait()
    load_x.wait()
    tail = pl.ds(local - 16, 16)

    def rim_copy():
        return remote(x_ref.at[tail], rim_in, x_sem.at[0], x_sem.at[1], {"seq": seq + 1})

    @pl.when(seq < seq_n - 1)
    def _():
        rim_copy().start()

    def f_copy(c):
        return remote(f_out.at[c], f_in.at[c], f_sem.at[0, c], f_sem.at[1, c], {"seq": seq + 1})

    def b_copy(c):
        return remote(b_out.at[c], b_in.at[c], b_sem.at[0, c], b_sem.at[1, c], {"seq": seq - 1})

    def advance(c):
        state = f_in[c].astype(F32)
        for b in range(blocks):
            state = whole[b, 0:1, lanes(c)] * state + push[b, c]
        f_out[c] = state.astype(BF16)

    def retreat(c):
        state = b_in[c].astype(F32)
        for b in reversed(range(blocks)):
            state = whole[b, 0:1, lanes(c)] * state + pull[b, c]
        b_out[c] = state.astype(BF16)

    outs_t = [jnp.transpose(co_ref[spans(b), :].astype(F32)).astype(BF16) for b in range(blocks)]

    @pl.when(seq == seq_n - 1)
    def _():
        b_in[...] = jnp.zeros(b_in.shape, BF16)

    def pulled(g, carry):
        e = spread(g)
        for b in range(blocks):
            scaled = (dot(packs[0, spans(b), :], e) * og_ref[spans(b), lanes(g)].astype(F32)).astype(BF16)
            sg[spans(b), lanes(g)] = scaled
            pull[b, g] = dot(outs_t[b], scaled)

        @pl.when((seq == seq_n - 1) & (seq > 0))
        def _():
            retreat(g)
            b_copy(g).start()

        return carry

    lax.fori_loop(0, groups, pulled, 0)

    xpad[pl.ds(8, local), :] = x_ref[...].astype(F32)

    @pl.when(seq == 0)
    def _():
        xpad[pl.ds(0, 8), :] = jnp.zeros((8, channels), F32)
        f_in[...] = jnp.zeros(f_in.shape, BF16)

    @pl.when(seq > 0)
    def _():
        rim_copy().wait_recv()
        xpad[pl.ds(0, 8), :] = rim_in[...].astype(F32)[8:]

    ins_t = [jnp.transpose(bi_ref[spans(b), :].astype(F32)).astype(BF16) for b in range(blocks)]

    def shifted(b, k, g):
        return xpad[pl.ds(8 + b * BLOCK - (taps - 1) + k, BLOCK), lanes(g)]

    def pushed(g):
        e = spread(g)
        for b in range(blocks):
            mixed = w_ref[0:1, lanes(g)] * shifted(b, 0, g)
            for k in range(1, taps):
                mixed = mixed + w_ref[k : k + 1, lanes(g)] * shifted(b, k, g)
            gate = 0.5 + 0.5 * jnp.tanh(0.5 * mixed)
            gain = dot(packs[2, spans(b), :], e)
            end = dot(packs[1, spans(b), :], e)
            act = (mixed * gate * gain).astype(BF16)
            scan[spans(b), lanes(g)] = act
            gs[spans(b), lanes(g)] = gain * gate * (1.0 + mixed * (1.0 - gate))
            ee[spans(b), lanes(g)] = end
            scaled = (end * act.astype(F32)).astype(BF16)
            ss[spans(b), lanes(g)] = scaled
            push[b, g] = dot(ins_t[b], scaled)

        @pl.when((seq == 0) & (seq < seq_n - 1))
        def _():
            advance(g)
            f_copy(g).start()


    hop = 5

    def work(p):
        pair = pl.ds(pl.multiple_of(p * 128, 128), 128)
        for b in range(blocks):
            scan_p = scan[spans(b), pair]
            grad_p = og_ref[spans(b), pair]
            side = lax.div(iota((BLOCK, 128), 1), width)
            total = jnp.zeros((BLOCK, 128), F32)
            weights = wsum[b]
            for j in range(per):
                h = p * per + j
                scan_h = jnp.where(side == j, scan_p, jnp.zeros_like(scan_p))
                grad_h = jnp.where(side == j, grad_p, jnp.zeros_like(grad_p))
                scores = dot_lanes(scan_h, grad_p)
                column = colb[h, spans(b), :]
                column = jnp.concatenate([column] * (BLOCK // 128), axis=1)
                decay = jnp.exp((rowb[b, h] - column) + mask[b])
                weights = weights + scores * decay
                total = total + dot((inner[b] * decay).astype(BF16), grad_h)
            wsum[b] = weights
            sgrad[spans(b), pair] = total

    def step(k, carry):
        @pl.when(k < groups)
        def _():
            pushed(k)

        @pl.when((k >= groups) & (k < groups + pairs))
        def _():
            work(k - groups)

        c_f = k - hop * seq

        @pl.when((seq > 0) & (seq < seq_n - 1) & (c_f >= 0) & (c_f < groups))
        def _():
            f_copy(c_f).wait_recv()
            advance(c_f)
            f_copy(c_f).start()

        c_b = k - hop * (seq_n - 2 - seq)

        @pl.when((seq > 0) & (seq < seq_n - 1) & (c_b >= 0) & (c_b < groups))
        def _():
            b_copy(c_b).wait_recv()
            retreat(c_b)
            b_copy(c_b).start()

        return carry

    steps = max(groups + pairs, hop * max(seq_n - 2, 0) + groups)
    lax.fori_loop(0, steps, step, 0)

    def c_copy(index, step):
        return remote(
            cbuf.at[chan, index], cbuf.at[chan, index],
            c_send.at[index, step], c_recv.at[index, step], peer(step),
        )

    def out_stage():
        @pl.when(seq == seq_n - 1)
        def _():
            @pl.when(seq > 0)
            def _():
                for c in range(groups):
                    f_copy(c).wait_recv()

        acc = []
        for b in range(blocks):
            acc.append(dot(jnp.transpose(wsum[b]).astype(BF16), bi_ref[spans(b), :]))
        for c in range(groups):
            part = slice(c * GROUP, (c + 1) * GROUP)
            state = f_in[c]
            for b in range(blocks):
                acc[b] = acc[b] + dot_lanes(sg[spans(b), part], state)
                if b < blocks - 1:
                    state = (whole[b, 0:1, part] * state.astype(F32) + push[b, c]).astype(BF16)
        for b in range(blocks):
            cbuf[chan, 1, spans(b), :] = acc[b].astype(BF16)
        for step_c in range(1, chan_n):
            c_copy(1, step_c).start()

    def in_stage():
        @pl.when(seq == 0)
        def _():
            @pl.when(seq < seq_n - 1)
            def _():
                for c in range(groups):
                    b_copy(c).wait_recv()

        acc = []
        for b in range(blocks):
            acc.append(dot(wsum[b].astype(BF16), co_ref[spans(b), :]))
        for c in range(groups):
            part = slice(c * GROUP, (c + 1) * GROUP)
            state = b_in[c]
            for b in reversed(range(blocks)):
                lead[b, c] = state
                acc[b] = acc[b] + dot_lanes(ss[spans(b), part], state)
                if b > 0:
                    state = (whole[b, 0:1, part] * state.astype(F32) + pull[b, c]).astype(BF16)
        for b in range(blocks):
            cbuf[chan, 0, spans(b), :] = acc[b].astype(BF16)
        for step_c in range(1, chan_n):
            c_copy(0, step_c).start()

    early = seq < seq_n // 2

    @pl.when(early)
    def _():
        out_stage()

    in_stage()

    def mixed_grads(b, g, carry):
        cross = dot(bi_ref[spans(b), :], lead[b, g])
        grad = sgrad[spans(b), lanes(g)] + ee[spans(b), lanes(g)] * cross
        rounded = (gs[spans(b), lanes(g)] * grad).astype(BF16)
        if b == 0:
            mg_out[:, lanes(g)] = rounded[:16]
        wide = rounded.astype(F32)
        mgpad[spans(b), lanes(g)] = wide
        for k in range(taps):
            row = jnp.sum(wide * shifted(b, k, g), axis=0, keepdims=True)
            if b > 0:
                row = row + wbuf[mine, pl.ds(k, 1), lanes(g)]
            wbuf[mine, pl.ds(k, 1), lanes(g)] = row
        return carry

    def m_copy():
        return remote(mg_out, mg_in, m_sem.at[0], m_sem.at[1], {"seq": seq - 1})

    def w_copy(step):
        return remote(wbuf.at[mine], wbuf.at[mine], w_send.at[step], w_recv.at[step], member(step))

    lax.fori_loop(0, groups, functools.partial(mixed_grads, 0), 0, unroll=4)

    @pl.when(seq > 0)
    def _():
        m_copy().start()

    for b in range(1, blocks):
        lax.fori_loop(0, groups, functools.partial(mixed_grads, b), 0, unroll=4)

    def w_start(step, carry):
        w_copy(step).start()
        return carry

    lax.fori_loop(1, team, w_start, 0)

    @pl.when(jnp.logical_not(early))
    def _():
        out_stage()

    def input_grads(b, g, carry):
        total = jnp.zeros((BLOCK, GROUP), F32)
        for k in range(taps):
            total = total + w_ref[k : k + 1, lanes(g)] * mgpad[
                pl.ds(b * BLOCK + taps - 1 - k, BLOCK), lanes(g)
            ]
        ig_ref[spans(b), lanes(g)] = total.astype(BF16)
        return carry

    for b in range(blocks):
        if b == blocks - 1:
            @pl.when(seq == seq_n - 1)
            def _():
                mgpad[pl.ds(local, 8), :] = jnp.zeros((8, channels), F32)

            @pl.when(seq < seq_n - 1)
            def _():
                m_copy().wait_recv()
                mgpad[pl.ds(local, 8), :] = mg_in[...].astype(F32)[:8]

        lax.fori_loop(0, groups, functools.partial(input_grads, b), 0, unroll=4)

    for index, ref in enumerate((sig_ref, sog_ref)):
        for step_c in range(1, chan_n):
            c_copy(index, step_c).wait_recv()
        total = cbuf[0, index].astype(F32)
        for source in range(1, chan_n):
            total = total + cbuf[source, index].astype(F32)
        ref[...] = total

    def w_wait(step, carry):
        w_copy(step).wait_recv()
        return carry

    lax.fori_loop(1, team, w_wait, 0)
    total = lax.fori_loop(
        0, team, lambda i, t: t + wbuf[i], jnp.zeros((taps, channels), F32)
    )
    wg_ref[...] = total * (1.0 / math.sqrt(dp_n * seq_n * local))

    def w_left(step, carry):
        w_copy(step).wait_send()
        return carry

    lax.fori_loop(1, team, w_left, 0)
    for index in range(2):
        for step_c in range(1, chan_n):
            c_copy(index, step_c).wait_send()

    @pl.when(seq < seq_n - 1)
    def _():
        rim_copy().wait_send()
        for c in range(groups):
            f_copy(c).wait_send()

    @pl.when(seq > 0)
    def _():
        m_copy().wait_send()
        for c in range(groups):
            b_copy(c).wait_send()


def write_out(*refs):
    sems = refs[-1]
    copies = [pltpu.make_async_copy(refs[i], refs[i + 4], sems.at[i]) for i in range(4)]
    for copy in copies:
        copy.start()
    for copy in copies:
        copy.wait()


def per_device(
    sizes, conv_input, conv_weight, log_decay, state_in, state_out, out_grad, lengths, segment_starts
):
    seq_n, chan_n, dp_n = sizes
    batch, local, channels = conv_input.shape
    heads = log_decay.shape[2]
    states = state_in.shape[2]
    taps = conv_weight.shape[0]
    blocks = local // BLOCK
    groups = channels // GROUP
    team = seq_n * dp_n
    vmem = pl.BlockSpec(memory_space=pltpu.VMEM)
    hbm = pl.BlockSpec(memory_space=pltpu.HBM)
    smem = pl.BlockSpec(memory_space=pltpu.SMEM)
    dma = pltpu.SemaphoreType.DMA
    flat = (local, channels)
    states_shape = (groups, states, GROUP)
    outs = pl.pallas_call(
        functools.partial(kernel, seq_n, chan_n, dp_n),
        out_shape=(
            pltpu.VMEM(flat, BF16),
            pltpu.VMEM((local, states), F32),
            pltpu.VMEM((local, states), F32),
            pltpu.VMEM((taps, channels), F32),
        ),
        in_specs=[hbm] + [vmem] * 4 + [hbm] + [smem] * 2,
        out_specs=[vmem] * 4,
        scratch_shapes=[
            pltpu.VMEM(flat, BF16),
            pltpu.VMEM(flat, BF16),
            dma((2,)),
            pltpu.VMEM((16, channels), BF16),
            pltpu.VMEM((local + 8, channels), F32),
            pltpu.VMEM((local + 8, channels), F32),
            pltpu.VMEM(flat, F32),
            pltpu.VMEM(flat, F32),
            pltpu.VMEM(flat, F32),
            pltpu.VMEM((heads, local, 128), F32),
            pltpu.VMEM((blocks, heads, 1, BLOCK), F32),
            pltpu.VMEM((blocks, BLOCK, BLOCK), F32),
            pltpu.VMEM((blocks, BLOCK, BLOCK), F32),
            pltpu.VMEM((blocks, BLOCK, BLOCK), F32),
            pltpu.VMEM((3, local, 2 * heads), BF16),
            pltpu.VMEM((blocks, 8, channels), F32),
            pltpu.VMEM(flat, BF16),
            pltpu.VMEM(flat, BF16),
            pltpu.VMEM(flat, BF16),
            pltpu.VMEM((blocks,) + states_shape, F32),
            pltpu.VMEM((blocks,) + states_shape, F32),
            pltpu.VMEM((blocks,) + states_shape, BF16),
            pltpu.VMEM(states_shape, BF16),
            pltpu.VMEM(states_shape, BF16),
            pltpu.VMEM(states_shape, BF16),
            pltpu.VMEM(states_shape, BF16),
            pltpu.VMEM((chan_n, 2, local, states), BF16),
            pltpu.VMEM((16, channels), BF16),
            pltpu.VMEM((16, channels), BF16),
            pltpu.VMEM((team, taps, channels), F32),
            dma((2,)),
            dma((2, groups)),
            dma((2, groups)),
            dma((2,)),
            dma((2, chan_n)),
            dma((2, chan_n)),
            dma((team,)),
            dma((team,)),
        ],
        compiler_params=pltpu.CompilerParams(
            collective_id=0, has_side_effects=True, vmem_limit_bytes=61 * 1024 * 1024
        ),
        cost_estimate=pl.CostEstimate(
            flops=4_000_000_000, bytes_accessed=4_000_000, transcendentals=4_000_000
        ),
    )(
        conv_input[0], conv_weight, jnp.transpose(log_decay[0]), state_in[0], state_out[0], out_grad[0],
        lengths, segment_starts,
    )
    outs = pl.pallas_call(
        write_out,
        out_shape=(
            jax.ShapeDtypeStruct(flat, BF16),
            jax.ShapeDtypeStruct((local, states), F32),
            jax.ShapeDtypeStruct((local, states), F32),
            jax.ShapeDtypeStruct((taps, channels), F32),
        ),
        in_specs=[vmem] * 4,
        out_specs=[hbm] * 4,
        scratch_shapes=[dma((4,))],
        compiler_params=pltpu.CompilerParams(vmem_limit_bytes=8 * 1024 * 1024),
    )(*outs)
    return (outs[0][None], outs[1][None], outs[2][None], outs[3])


def solution(mesh):
    sizes = (mesh.shape["seq"], mesh.shape["chan"], mesh.shape["dp"])
    placed = (
        P(("groups", "dp"), "seq", "chan"),
        P(None, "chan"),
        P(("groups", "dp"), "seq", "chan"),
        P(("groups", "dp"), "seq", None),
        P(("groups", "dp"), "seq", None),
        P(("groups", "dp"), "seq", "chan"),
        P(("groups", "dp")),
        P(("groups", "dp"), None),
    )
    return jax.shard_map(
        functools.partial(per_device, sizes),
        mesh=mesh,
        in_specs=placed,
        out_specs=(
            P(("groups", "dp"), "seq", "chan"),
            P(("groups", "dp"), "seq", None),
            P(("groups", "dp"), "seq", None),
            P("groups", "chan"),
        ),
        check_vma=False,
    )
```
